512 devices in a mesh: dp: 16 (over x, y_lo), seq: 32 (over y_hi, z, core).
Axes of the slice: x: 4, y: 8 (y_hi: 2, y_lo: 4; y = y_hi * 4 + y_lo), z: 8, core: 2. Of those that a mesh axis runs over, the one named last changes fastest.
Arguments:
- inputs: bfloat16 [16, 8192, 768], P('dp', 'seq'), may hold values from -11 to 11
- gain: float32 [768], replicated, may hold values from 0.1 to 1.9
- shift: float32 [768], replicated, may hold values from -1 to 1
- kernel: bfloat16 [768, 3, 768], P('seq'), may hold values from -0.21875 to 0.21875
- cotangent: bfloat16 [16, 8192, 768], P('dp', 'seq'), may hold values from -6 to 6
Outputs:
- output: bfloat16 [16, 8192, 768], P('dp', 'seq')
- grad_in: bfloat16 [16, 8192, 768], P('dp', 'seq')
- weight_grad: float32 [768, 3, 768], P('seq')
- gain_grad: float32 [768], replicated
- shift_grad: float32 [768], replicated
The draws below stay inside these ranges and needn't reach their ends.
All inputs are finite; a program needn't handle non-finite values.
Results may differ from the reference program's by a relative error of at most 0.008.
Values may be sent and summed in bfloat16 or wider, within the bound.
No kernel may reach another device: no remote copies, remote signals or barrier semaphores. Data moves between devices by JAX's collectives and lax.ppermute only.
A program may use at most 64 MiB of HBM per device.

```python
import math
import jax
import jax.numpy as jnp
from jax import lax

C = 768
L_DEV = 256
DILATION_STEP = 256
BATCH = 16
SEQUENCE_LENGTH = 8192
N_SEQ = 32


def block_pattern(key, block_total, channels):
    bit_count = max(1, (block_total - 1).bit_length())
    amplitude = 2.25 / max(bit_count, 9)
    signs = 2.0 * jax.random.bernoulli(key, 0.5, (bit_count, channels)).astype(jnp.float32) - 1.0
    block_ids = jnp.arange(block_total, dtype=jnp.int32)
    pattern = jnp.zeros((block_total, channels), jnp.float32)
    for level in range(bit_count):
        bit_value = jnp.bitwise_and(jnp.right_shift(block_ids, level), 1).astype(jnp.float32)
        pattern = pattern + amplitude * (1.0 - 2.0 * bit_value)[:, None] * signs[level][None, :]
    return pattern


def draw_inputs(key, part):
    key = jax.random.fold_in(key, 11)
    key_rough, key_channel, key_offset, key_rows, key_blocks = jax.random.split(key, 5)
    rough_part = jnp.clip(jax.random.normal(key_rough, (BATCH, SEQUENCE_LENGTH, C), jnp.float32), -3.0, 3.0)
    scale_per_channel = jnp.exp(jax.random.uniform(key_channel, (C,), jnp.float32, math.log(0.4), math.log(2.5)))
    offset = jax.random.uniform(key_offset, (C,), jnp.float32, -1.0, 1.0)
    row_scale = jnp.exp(jax.random.uniform(key_rows, (BATCH, SEQUENCE_LENGTH, 1), jnp.float32, math.log(0.5), math.log(2.0)))
    blocks_per_sequence = SEQUENCE_LENGTH // L_DEV
    pattern = block_pattern(key_blocks, BATCH * blocks_per_sequence, C)
    pattern = jnp.broadcast_to(pattern.reshape(BATCH, blocks_per_sequence, 1, C), (BATCH, blocks_per_sequence, L_DEV, C)).reshape(BATCH, SEQUENCE_LENGTH, C)
    position = (jnp.arange(BATCH, dtype=jnp.float32)[:, None] * SEQUENCE_LENGTH + jnp.arange(SEQUENCE_LENGTH, dtype=jnp.float32)[None, :]) / (BATCH * SEQUENCE_LENGTH)
    ramp_scale = jnp.sqrt(1.0 + 2.0 * position)[:, :, None]
    return (0.2 * ramp_scale * row_scale * scale_per_channel * (rough_part + offset + pattern)).astype(jnp.bfloat16)


def draw_cotangent(key, part):
    key = jax.random.fold_in(key, 23)
    key_noise, key_mean = jax.random.split(key, 2)
    noise = jnp.clip(jax.random.normal(key_noise, (BATCH, SEQUENCE_LENGTH, C), jnp.float32), -4.0, 4.0)
    channel_mean = 0.25 * jnp.clip(jax.random.normal(key_mean, (C,), jnp.float32), -3.0, 3.0)
    return (noise + channel_mean).astype(jnp.bfloat16)


def steps_of(key, shape, shards, low, high):
    level, own = 1.0, jax.random.fold_in(key, 6)
    for dim, blocks in shards:
        steps = jnp.exp(jax.random.uniform(jax.random.fold_in(own, dim), (blocks,), jnp.float32, low / len(shards), high / len(shards)))
        level = level * jnp.repeat(steps, shape[dim] // blocks).reshape([-1 if axis == dim else 1 for axis in range(len(shape))])
    return level


def gaussian(key, dims, deviation, limit, cuts=(), kind=jnp.bfloat16):
    values = jax.random.normal(key, dims, jnp.float32) * deviation
    if len(cuts) > 0:
        values = steps_of(key, dims, cuts, -0.22, 0.18) * values
    return jnp.clip(values, min=-limit, max=limit).astype(kind)


def setup_inputs(seed: int = 0) -> dict:
    seeds = jax.random.split(jax.random.key(seed), 6)
    inputs = draw_inputs(jax.random.fold_in(seeds[5], 71), 0)
    gain = jnp.clip(1.0 + 0.18 * jax.random.normal(seeds[1], (C,), jnp.float32), 0.1, 1.9)
    shift = jnp.clip(jax.random.uniform(seeds[2], (C,), jnp.float32, -1.0, 1.0), -1.0, 1.0)
    kernel = gaussian(seeds[3], (C, 3, C), C ** -0.5, 0.21875, ((0, 32),))
    cotangent = draw_cotangent(jax.random.fold_in(seeds[5], 71), 0)
    return {"inputs": inputs, "gain": gain, "shift": shift, "kernel": kernel, "cotangent": cotangent}


def gelu_exact(values):
    return jax.nn.gelu(values, approximate=False)

def neighbours(input_sequence):
    zero_border = jnp.zeros((DILATION_STEP, input_sequence.shape[1]), input_sequence.dtype)
    lower_sequence = jnp.concatenate([zero_border, input_sequence[:SEQUENCE_LENGTH - DILATION_STEP]], axis=0)
    upper_sequence = jnp.concatenate([input_sequence[DILATION_STEP:], zero_border], axis=0)
    return (lower_sequence, upper_sequence)

def reference(inputs, gain, shift, kernel, cotangent):
    count_all = BATCH * SEQUENCE_LENGTH
    norm_scale = 1.0 / jnp.sqrt(jnp.float32(count_all))
    col_sum = lax.optimization_barrier(jnp.sum(lax.map(lambda seq_in: lax.optimization_barrier(jnp.sum(seq_in.astype(jnp.float32), axis=0)), inputs), axis=0))
    col_mean = col_sum / count_all

    def centred_sum(seq_in):
        centred = seq_in.astype(jnp.float32) - col_mean
        return lax.optimization_barrier(jnp.sum(centred * centred, axis=0))
    variance = lax.optimization_barrier(jnp.sum(lax.map(centred_sum, inputs), axis=0)) / count_all
    inv_std = lax.rsqrt(variance + 1e-05)
    kernel_full = kernel.astype(jnp.float32)

    def forward_one(pair):
        seq_in, seq_cot = pair
        values = seq_in.astype(jnp.float32)
        normed = (values - col_mean) * inv_std
        pre_act = gain * normed + shift
        activated = lax.optimization_barrier(gelu_exact(pre_act).astype(jnp.bfloat16))
        below_act, above_act = neighbours(activated)
        act_stack = jnp.stack([below_act, activated, above_act], axis=1).astype(jnp.float32)
        mixed_sum = jnp.einsum('lki,ikc->lc', act_stack, kernel_full)
        output = (values + mixed_sum).astype(jnp.bfloat16)
        below_cot, upper_gradient = neighbours(seq_cot)
        cot_stack = jnp.stack([upper_gradient, seq_cot, below_cot], axis=1).astype(jnp.float32)
        back_proj = jnp.einsum('lkc,ikc->li', cot_stack, kernel_full)
        unused, tangent = jax.vjp(gelu_exact, pre_act)
        pre_grad = tangent(back_proj)[0]
        shift_part = lax.optimization_barrier(jnp.sum(pre_grad, axis=0))
        gain_part = lax.optimization_barrier(jnp.sum(pre_grad * normed, axis=0))
        blocks_act = act_stack.reshape(N_SEQ, L_DEV, 3, C)
        blocks_cot = seq_cot.astype(jnp.float32).reshape(N_SEQ, L_DEV, C)
        terms = jnp.einsum('slki,slc->sikc', blocks_act, blocks_cot) * norm_scale
        rounded = lax.optimization_barrier(terms.astype(jnp.bfloat16))
        weight_part = lax.optimization_barrier(jnp.sum(rounded.astype(jnp.float32), axis=0))
        return (output, pre_grad, shift_part, gain_part, weight_part)
    output, pre_grads, shift_parts, gain_parts, weight_parts = lax.map(forward_one, (inputs, cotangent))
    shift_total = lax.optimization_barrier(jnp.sum(shift_parts, axis=0))
    gain_total = lax.optimization_barrier(jnp.sum(gain_parts, axis=0))

    def input_grad(triple):
        seq_in, seq_cot, pre_grad = triple
        normed = (seq_in.astype(jnp.float32) - col_mean) * inv_std
        bn_grad = gain * inv_std * (pre_grad - shift_total / count_all - normed * gain_total / count_all)
        return (seq_cot.astype(jnp.float32) + bn_grad).astype(jnp.bfloat16)
    grad_in = lax.map(input_grad, (inputs, cotangent, pre_grads))
    weight_grad = lax.optimization_barrier(jnp.sum(weight_parts, axis=0))
    return (output, grad_in, weight_grad, gain_total * norm_scale, shift_total * norm_scale)
```

```python
import jax
import jax.numpy as jnp
from jax import lax
from jax.sharding import Mesh, PartitionSpec as P

F32 = jnp.float32
BF16 = jnp.bfloat16
AXES = ("x", "yl", "yh", "z", "c")
NX, NYL, NYH, NZ, NC = 4, 4, 2, 8, 2
SEQ = ("yh", "z", "c")
SEQ_N = NYH * NZ * NC
C = 768
L = 256
ROWS = 24
PIECE = 27
SQRT_HALF = 0.7071067811865476
INV_SQRT_2PI = 0.3989422804014327


def broadcast_all(value, axes):
    n = lax.axis_size(axes)
    return lax.all_to_all(jnp.broadcast_to(value[None], (n,) + value.shape), axes, 0, 0, tiled=True)


def merge_stats(parts, count):
    sums, squares = parts[:, 0], parts[:, 1]
    n = parts.shape[0]
    total = jnp.sum(sums, axis=0)
    off = sums / count - total / (count * n)
    return jnp.stack([total, jnp.sum(squares, axis=0) + count * jnp.sum(off * off, axis=0)])


def split(value):
    high = lax.reduce_precision(value, 8, 7)
    return high.astype(BF16), (value - high).astype(BF16)


def body(inputs, gain, shift, kernel, cotangent):
    xi, yl, yh, zi, ci = (lax.axis_index(a) for a in AXES)
    count_all = L * SEQ_N * NX * NYL
    norm_scale = 1.0 / jnp.sqrt(jnp.float32(count_all))
    inputs, cotangent = inputs[0], cotangent[0]
    values = inputs.astype(F32)

    swap_y = []
    for l in range(NYL):
        for h in range(NYH):
            y = 7 - (h * NYL + l)
            swap_y.append((l * NYH + h, (y % NYL) * NYH + y // NYL))
    own = kernel.reshape(ROWS * 3, C)
    other = lax.ppermute(own, ("yl", "yh"), swap_y)
    first = yh == 0
    both = jnp.stack([jnp.where(first, own, other), jnp.where(first, other, own)])
    kernel_c = lax.all_gather(both, "z", axis=0, tiled=False)

    pair = jnp.concatenate([cotangent, inputs], axis=0)
    swap_c = [(0, 1), (1, 0)]
    mate = lax.ppermute(pair, "c", swap_c)
    outer = lax.ppermute(
        pair, SEQ, [(i, j) for i in range(1, SEQ_N - 1, 2) for i, j in ((i, i + 1), (i + 1, i))]
    )
    far = lax.ppermute(outer[:L], "c", swap_c)

    total = jnp.sum(values, axis=0)
    off = values - total / L
    stats = jnp.stack([total, jnp.sum(off * off, axis=0)])
    stats = merge_stats(broadcast_all(stats, ("x", "yl", "yh")), L)
    stats = merge_stats(broadcast_all(stats, ("z", "c")), L * NX * NYL * NYH)
    col_mean = stats[0] / count_all
    inv_std = lax.rsqrt(stats[1] / count_all + 1e-05)

    def activate(block):
        normed = (block.astype(F32) - col_mean) * inv_std
        v = gain * normed + shift
        half = 0.5 * (1.0 + lax.erf(v * SQRT_HALF))
        return normed, v, half

    normed, v, half = activate(inputs)
    act = (v * half).astype(BF16)
    slope = half + v * (INV_SQRT_2PI * jnp.exp(-0.5 * v * v))
    _, v_m, half_m = activate(mate[L:])
    act_mate = (v_m * half_m).astype(BF16)
    _, v_o, half_o = activate(outer[L:])
    seq = (yh * NZ + zi) * NC + ci
    has_outer = jnp.logical_and(seq > 0, seq < SEQ_N - 1)
    act_outer = jnp.where(has_outer, v_o * half_o, 0.0).astype(BF16)

    low = ci == 0
    cot_mate, cot_outer = mate[:L], outer[:L]
    q0 = jnp.where(low, cot_outer, far)
    q1 = jnp.where(low, cotangent, cot_mate)
    q2 = jnp.where(low, cot_mate, cotangent)
    q3 = jnp.where(low, far, cot_outer)
    quad = jnp.concatenate([q0, q1, q2, q3], axis=0)
    act_pair = jnp.concatenate([jnp.where(low, act, act_mate), jnp.where(low, act_mate, act)], axis=0)

    order = jnp.arange(C // 2)
    quarter, owner, row = order // 96, (order // 6) % 16, order % 6
    source = (owner * NC + ci) * ROWS + quarter * 6 + row
    select = (jnp.arange(C)[:, None] == source[None, :]).astype(BF16)
    act_sel = jnp.dot(act_pair, select, preferred_element_type=F32).astype(BF16)
    terms = jnp.concatenate(
        [
            jnp.einsum("li,lc->ic", act_sel, quad[(2 - k) * L : (4 - k) * L], preferred_element_type=F32)
            for k in range(3)
        ],
        axis=1,
    )
    terms = (terms * norm_scale).astype(BF16)
    terms = lax.all_to_all(terms.reshape(NX, 96, 3 * C), "x", 0, 0, tiled=True)
    terms = jnp.sum(terms.astype(F32), axis=0).astype(BF16)
    terms = terms.reshape(NYH, NZ, NYL, PIECE, 128).transpose(2, 0, 1, 3, 4).reshape(64, PIECE, 128)

    kernel_o = lax.ppermute(kernel_c, "c", swap_c)
    k0 = jnp.where(low, kernel_c, kernel_o)
    k1 = jnp.where(low, kernel_o, kernel_c)
    full = jnp.stack([k0, k1]).transpose(2, 1, 0, 3, 4).reshape(C, 3, C)

    cots = jnp.stack(
        [jnp.where(low, q2, q3), cotangent, jnp.where(low, q0, q1)], axis=1
    )
    back_proj = jnp.einsum("lkc,ikc->li", cots, full, preferred_element_type=F32)
    pre_grad = back_proj * slope
    totals = jnp.stack([jnp.sum(pre_grad, axis=0), jnp.sum(pre_grad * normed, axis=0)])
    totals = lax.psum(totals, "c")
    high, rest = split(totals)
    packed = jnp.concatenate([high.reshape(12, 128), rest.reshape(12, 128)], axis=0)
    message = jnp.concatenate([terms, jnp.broadcast_to(packed[None], (64, 24, 128))], axis=1)
    got = lax.all_to_all(message, ("yl", "yh", "z"), 0, 0, tiled=True)
    got = jnp.sum(got.astype(F32), axis=0)
    totals = got[PIECE : PIECE + 12] + got[PIECE + 12 :]
    high, rest = split(totals)
    packed = jnp.concatenate([got[:PIECE].astype(BF16), high, rest], axis=0)
    got = broadcast_all(packed, ("x", "yl")).astype(F32)
    weight_grad = got[:, :PIECE].reshape(ROWS, 3, C)
    totals = jnp.sum(got.reshape(NX, NYL, PIECE + 24, 128)[:, 0, PIECE:], axis=0)
    totals = (totals[:12] + totals[12:]).reshape(2, C)
    shift_total, gain_total = totals[0], totals[1]

    before = jnp.where(low, act_outer, act_mate)
    after = jnp.where(low, act_mate, act_outer)
    acts = jnp.stack([before, act, after], axis=1)
    mixed_sum = jnp.einsum("lki,ikc->lc", acts, full, preferred_element_type=F32)
    output = (values + mixed_sum).astype(BF16)
    bn_grad = gain * inv_std * (pre_grad - shift_total / count_all - normed * gain_total / count_all)
    grad_in = (cotangent.astype(F32) + bn_grad).astype(BF16)
    return (output[None], grad_in[None], weight_grad, gain_total * norm_scale, shift_total * norm_scale)


def solution(mesh):
    split_mesh = Mesh(mesh.devices.reshape(NX, NYL, NYH, NZ, NC), AXES)
    rows = P(("x", "yl"), SEQ, None)
    return jax.shard_map(
        body,
        mesh=split_mesh,
        in_specs=(rows, P(), P(), P(SEQ, None, None), rows),
        out_specs=(rows, rows, P(SEQ, None, None), P(), P()),
        check_vma=False,
    )
```

```python
import jax
import jax.numpy as jnp
from jax import lax
from jax.experimental import pallas as pl
from jax.experimental.pallas import tpu as pltpu
from jax.sharding import Mesh, PartitionSpec as P

F32 = jnp.float32
BF16 = jnp.bfloat16
AXES = ("x", "yl", "yh", "z", "c")
NX, NYL, NYH, NZ, NC = 4, 4, 2, 8, 2
SEQ = ("yh", "z", "c")
SEQ_N = NYH * NZ * NC
C = 768
HALF = C // 2
L = 256
ROWS = 24
PIECE = 27
TOT = 24
SQRT_HALF = 0.7071067811865476
INV_SQRT_2PI = 0.3989422804014327
PARAMS = pltpu.CompilerParams(vmem_limit_bytes=40 * 1024 * 1024)


def broadcast_all(value, axes):
    n = lax.axis_size(axes)
    return lax.all_to_all(jnp.broadcast_to(value[None], (n,) + value.shape), axes, 0, 0, tiled=True)


def merge_stats(parts, count):
    sums, squares = parts[:, 0], parts[:, 1]
    n = parts.shape[0]
    total = jnp.sum(sums, axis=0)
    off = sums / count - total / (count * n)
    return jnp.stack([total, jnp.sum(squares, axis=0) + count * jnp.sum(off * off, axis=0)])


def pack(totals):
    high = lax.reduce_precision(totals, 8, 7)
    return jnp.concatenate([high.astype(BF16), (totals - high).astype(BF16)], axis=0).reshape(TOT, 128)


def unpack(packed):
    return (packed[: TOT // 2] + packed[TOT // 2 :]).reshape(2, C)


def by_taps(ref, tap):
    return ref[:, tap].reshape(HALF, C)


def back_kernel(q0, q1, q2, kc, ko, sc, so, slope, normed, pre_grad, totals):
    total = jnp.zeros((L, C), F32)
    for kern, sel in ((kc, sc), (ko, so)):
        part = jnp.zeros((L, HALF), F32)
        for tap, q in enumerate((q0, q1, q2)):
            part += lax.dot_general(
                q[...], by_taps(kern, tap), (((1,), (1,)), ((), ())), preferred_element_type=F32
            )
        high = part.astype(BF16)
        low = (part - high.astype(F32)).astype(BF16)
        total += jnp.dot(high, sel[...], preferred_element_type=F32)
        total += jnp.dot(low, sel[...], preferred_element_type=F32)
    grad = total * slope[...]
    pre_grad[...] = grad
    totals[0:1] = jnp.sum(grad, axis=0, keepdims=True)
    totals[1:2] = jnp.sum(grad * normed[...], axis=0, keepdims=True)


def forward_kernel(a0, a1, a2, kc, ko, sc, so, inputs, output):
    total = inputs[...].astype(F32)
    for kern, sel in ((kc, sc), (ko, so)):
        for tap, a in enumerate((a0, a1, a2)):
            chosen = lax.dot_general(
                a[...], sel[...], (((1,), (1,)), ((), ())), preferred_element_type=F32
            ).astype(BF16)
            total += jnp.dot(chosen, by_taps(kern, tap), preferred_element_type=F32)
    output[...] = total.astype(BF16)


def cost(flops, size):
    return pl.CostEstimate(flops=flops, bytes_accessed=size, transcendentals=0)


def body(inputs, gain, shift, kernel, cotangent):
    xi, yl, yh, zi, ci = (lax.axis_index(a) for a in AXES)
    count_all = L * SEQ_N * NX * NYL
    norm_scale = 1.0 / jnp.sqrt(jnp.float32(count_all))
    inputs, cotangent = inputs[0], cotangent[0]
    values = inputs.astype(F32)
    low = ci == 0
    swap_c = [(0, 1), (1, 0)]

    swap_y = []
    for l in range(NYL):
        for h in range(NYH):
            y = 7 - (h * NYL + l)
            swap_y.append((l * NYH + h, (y % NYL) * NYH + y // NYL))
    own = kernel.transpose(1, 0, 2)
    other = lax.ppermute(own, ("yl", "yh"), swap_y)

    pair = jnp.concatenate([cotangent, inputs], axis=0)
    mate = lax.ppermute(pair, "c", swap_c)
    outer = lax.ppermute(
        pair, SEQ, [(i, j) for i in range(1, SEQ_N - 1, 2) for i, j in ((i, i + 1), (i + 1, i))]
    )
    far = lax.ppermute(outer[:L], "c", swap_c)

    total = jnp.sum(values, axis=0)
    off = values - total / L
    stats = jnp.stack([total, jnp.sum(off * off, axis=0)])
    stats = merge_stats(broadcast_all(stats, ("z", "c")), L)

    first = yh == 0
    both = jnp.concatenate([jnp.where(first, own, other), jnp.where(first, other, own)], axis=1)
    stats, both = lax.optimization_barrier((stats, both))
    kernel_c = broadcast_all(both, "z")

    stats = merge_stats(broadcast_all(stats, ("x", "yl", "yh")), L * NZ * NC)
    col_mean = stats[0] / count_all
    inv_std = lax.rsqrt(stats[1] / count_all + 1e-05)

    order = jnp.arange(HALF)
    quarter, owner, row = order // 96, (order // 6) % 16, order % 6
    source = (owner * NC + ci) * ROWS + quarter * 6 + row
    choose = source[None, :] == jnp.arange(C)[:, None]
    select = choose.astype(BF16)
    mate_in = mate[L:]
    in_pair = jnp.concatenate([jnp.where(low, inputs, mate_in), jnp.where(low, mate_in, inputs)], axis=0)
    in_sel = jnp.dot(in_pair, select, preferred_element_type=F32)
    vectors = jnp.stack([col_mean, inv_std, gain, shift])
    vectors = jnp.sum(jnp.where(choose[None], vectors[:, :, None], 0.0), axis=1)
    v = vectors[2] * ((in_sel - vectors[0]) * vectors[1]) + vectors[3]
    act_sel = (v * (0.5 * (1.0 + lax.erf(v * SQRT_HALF)))).astype(BF16)

    cot_mate, cot_outer = mate[:L], outer[:L]
    q0 = jnp.where(low, cot_outer, far)
    q1 = jnp.where(low, cotangent, cot_mate)
    q2 = jnp.where(low, cot_mate, cotangent)
    q3 = jnp.where(low, far, cot_outer)
    quad = jnp.concatenate([q0, q1, q2, q3], axis=0)
    terms = jnp.concatenate(
        [
            jnp.einsum("li,lc->ic", act_sel, quad[(2 - k) * L : (4 - k) * L], preferred_element_type=F32)
            for k in range(3)
        ],
        axis=1,
    )
    terms = (terms * norm_scale).astype(BF16)
    terms, held_in, held_outer, held_mate = lax.optimization_barrier((terms, inputs, outer[L:], mate[L:]))
    terms = lax.all_to_all(terms.reshape(NX, 96, 3 * C), "x", 0, 0, tiled=True)

    def activate(block):
        normed = (block.astype(F32) - col_mean) * inv_std
        v = gain * normed + shift
        return normed, v, 0.5 * (1.0 + lax.erf(v * SQRT_HALF))

    normed, v, half = activate(held_in)
    act = (v * half).astype(BF16)
    slope = half + v * (INV_SQRT_2PI * jnp.exp(-0.5 * v * v))
    _, v_m, half_m = activate(held_mate)
    act_mate = (v_m * half_m).astype(BF16)
    _, v_o, half_o = activate(held_outer)
    seq = (yh * NZ + zi) * NC + ci
    has_outer = jnp.logical_and(seq > 0, seq < SEQ_N - 1)
    act_outer = jnp.where(has_outer, v_o * half_o, 0.0).astype(BF16)

    kernel_o = lax.ppermute(kernel_c, "c", swap_c)
    gz, gy, gr = order // (NYH * ROWS), (order // ROWS) % NYH, order % ROWS
    channel = (gy * NZ + gz) * NC * ROWS + gr
    sel_c = ((channel + ci * ROWS)[:, None] == jnp.arange(C)[None]).astype(BF16)
    sel_o = ((channel + (1 - ci) * ROWS)[:, None] == jnp.arange(C)[None]).astype(BF16)

    pre_grad, totals = pl.pallas_call(
        back_kernel,
        out_shape=(jax.ShapeDtypeStruct((L, C), F32), jax.ShapeDtypeStruct((2, C), F32)),
        compiler_params=PARAMS,
        cost_estimate=cost(2 * L * C * C * 5, 8 * 1024 * 1024),
        name="back",
    )(jnp.where(low, q2, q3), cotangent, jnp.where(low, q0, q1), kernel_c, kernel_o, sel_c, sel_o, slope, normed)
    totals = lax.psum(totals, "c")

    terms = jnp.sum(terms.astype(F32), axis=0).astype(BF16)
    terms = terms.reshape(NYH, NZ, NYL, PIECE, 128).transpose(2, 0, 1, 3, 4).reshape(8, NZ * PIECE, 128)
    message = jnp.concatenate([terms, jnp.broadcast_to(pack(totals)[None], (8, TOT, 128))], axis=1)
    got = jnp.sum(lax.all_to_all(message, ("yl", "yh"), 0, 0, tiled=True).astype(F32), axis=0)
    terms, totals = got[: NZ * PIECE].astype(BF16), unpack(got[NZ * PIECE :])
    message = jnp.concatenate(
        [terms.reshape(NZ, PIECE, 128), jnp.broadcast_to(pack(totals)[None], (NZ, TOT, 128))], axis=1
    )
    got = jnp.sum(lax.all_to_all(message, "z", 0, 0, tiled=True).astype(F32), axis=0)
    message = jnp.concatenate([got[:PIECE].astype(BF16), pack(unpack(got[PIECE:]))], axis=0)
    got = broadcast_all(message, ("x", "yl")).astype(F32)
    weight_grad = got[:, :PIECE].reshape(ROWS, 3, C)
    totals = unpack(jnp.sum(got.reshape(NX, NYL, PIECE + TOT, 128)[:, 0, PIECE:], axis=0))
    shift_total, gain_total = totals[0], totals[1]

    output = pl.pallas_call(
        forward_kernel,
        out_shape=jax.ShapeDtypeStruct((L, C), BF16),
        compiler_params=PARAMS,
        cost_estimate=cost(2 * L * C * C * 6, 6 * 1024 * 1024),
        name="forward",
    )(
        jnp.where(low, act_outer, act_mate), act, jnp.where(low, act_mate, act_outer),
        kernel_c, kernel_o, sel_c, sel_o, inputs,
    )
    bn_grad = gain * inv_std * (pre_grad - shift_total / count_all - normed * gain_total / count_all)
    grad_in = (cotangent.astype(F32) + bn_grad).astype(BF16)
    return (output[None], grad_in[None], weight_grad, gain_total * norm_scale, shift_total * norm_scale)


def solution(mesh):
    split_mesh = Mesh(mesh.devices.reshape(NX, NYL, NYH, NZ, NC), AXES)
    rows = P(("x", "yl"), SEQ, None)
    return jax.shard_map(
        body,
        mesh=split_mesh,
        in_specs=(rows, P(), P(), P(SEQ, None, None), rows),
        out_specs=(rows, rows, P(SEQ, None, None), P(), P()),
        check_vma=False,
    )
```

```python
import jax
import jax.numpy as jnp
from jax import lax
from jax.experimental import pallas as pl
from jax.experimental.pallas import tpu as pltpu
from jax.sharding import Mesh, PartitionSpec as P

F32 = jnp.float32
BF16 = jnp.bfloat16
AXES = ("x", "yl", "yh", "z", "c")
NX, NYL, NYH, NZ, NC = 4, 4, 2, 8, 2
SEQ = ("yh", "z", "c")
SEQ_N = NYH * NZ * NC
C = 768
HALF = C // 2
L = 256
ROWS = 24
OWNERS = NYH * NZ
SUB = ROWS // NX
PIECE = 27
TOT = 24
MSG = 64
COUNT = L * SEQ_N * NX * NYL
NORM = float(COUNT) ** -0.5
SQRT_HALF = 0.7071067811865476
INV_SQRT_2PI = 0.3989422804014327
NT = (((1,), (1,)), ((), ()))
TN = (((0,), (0,)), ((), ()))


def call(kernel, out_shape, name, megabytes, flops=0, size=1 << 20, smem=False, scratch=()):
    specs = None
    params = pltpu.CompilerParams(vmem_limit_bytes=megabytes * 1024 * 1024)
    estimate = pl.CostEstimate(flops=flops, bytes_accessed=size, transcendentals=0)
    extra = {}
    if smem:
        extra["in_specs"] = [pl.BlockSpec(memory_space=pltpu.SMEM)] + [
            pl.BlockSpec(memory_space=pltpu.VMEM)
        ] * (smem - 1)
    return pl.pallas_call(
        kernel, out_shape=out_shape, compiler_params=params, cost_estimate=estimate, name=name,
        scratch_shapes=list(scratch), **extra,
    )


def spread(value, n):
    return jnp.broadcast_to(value[None], (n,) + value.shape)


def stats_kernel(inputs, message):
    values = inputs[...].astype(F32)
    total = jnp.sum(values, axis=0, keepdims=True)
    off = values - total / L
    squares = jnp.sum(off * off, axis=0, keepdims=True)
    message[...] = spread(jnp.concatenate([total, squares], axis=0), NZ * NC)


def merged(parts, count):
    sums, squares = parts[:, 0, :], parts[:, 1, :]
    n = sums.shape[0]
    total = jnp.sum(sums, axis=0, keepdims=True)
    off = sums / count - total / (count * n)
    return total, jnp.sum(squares, axis=0, keepdims=True) + count * jnp.sum(off * off, axis=0, keepdims=True)


def merge_kernel(parts, message):
    total, squares = merged(parts[...], L)
    message[...] = spread(jnp.concatenate([total, squares], axis=0), NX * NYL * NYH)


def one_hot(channels):
    rows = lax.broadcasted_iota(jnp.int32, (C, channels.shape[1]), 0)
    return jnp.where(rows == channels[...], 1.0, 0.0).astype(BF16)


def normalised(block, vectors):
    return (block - vectors[0:1]) * vectors[1:2]


def half_gate(v):
    return 0.5 * (1.0 + lax.erf(v * SQRT_HALF))


def terms_kernel(place, parts, gain, shift, source, inputs, mate, cot, outer, far, terms, vectors):
    total, squares = merged(parts[...], L * NZ * NC)
    mean = total / COUNT
    inv_std = lax.rsqrt(squares / COUNT + 1e-05)
    rows = jnp.concatenate([mean, inv_std, gain[...], shift[...]], axis=0)
    vectors[...] = rows
    pick = one_hot(source)
    chosen, rest = jnp.zeros((4, HALF), F32), rows
    for _ in range(3):
        part = rest.astype(BF16)
        chosen += jnp.dot(part, pick, preferred_element_type=F32)
        rest = rest - part.astype(F32)
    low = place[0] == 0
    both = jnp.concatenate([inputs[...], mate[L:]], axis=0)
    v = normalised(jnp.dot(both, pick, preferred_element_type=F32), chosen)
    v = chosen[2:3] * v + chosen[3:4]
    act = (v * half_gate(v)).astype(BF16)
    own, next_own, last_own = cot[...], mate[:L], outer[...]
    beyond = far[...]
    cots = (
        (jnp.where(low, next_own, last_own), jnp.where(low, beyond, own)),
        (own, next_own),
        (jnp.where(low, last_own, next_own), jnp.where(low, own, beyond)),
    )
    for tap, pair in enumerate(cots):
        block = lax.dot_general(act, jnp.concatenate(pair, axis=0), TN, preferred_element_type=F32)
        terms[:, tap * C : (tap + 1) * C] = (block * NORM).astype(BF16)


def by_tap(parts, tap):
    return jnp.concatenate([part[:, tap].reshape(-1, C) for part in parts], axis=0)


def back_kernel(place, vectors, inputs, mate, cot, outer, own, mine, theirs, channel, pre_grad, totals):
    low = place[0] == 0
    taps = (
        jnp.where(low, mate[:L], outer[...]),
        cot[...],
        jnp.where(low, outer[...], mate[:L]),
    )
    total = jnp.zeros((L, C), F32)
    for tap, q in enumerate(taps):
        total += lax.dot_general(q, by_tap((own, mine, theirs), tap), NT, preferred_element_type=F32)
    high = total.astype(BF16)
    rest = (total - high.astype(F32)).astype(BF16)
    pick = one_hot(channel)
    total = lax.dot_general(high, pick, NT, preferred_element_type=F32)
    total += lax.dot_general(rest, pick, NT, preferred_element_type=F32)
    rows = vectors[...]
    normed = normalised(inputs[...].astype(F32), rows)
    v = rows[2:3] * normed + rows[3:4]
    grad = total * (half_gate(v) + v * (INV_SQRT_2PI * jnp.exp(-0.5 * v * v)))
    pre_grad[...] = grad
    totals[...] = jnp.concatenate(
        [jnp.sum(grad, axis=0, keepdims=True), jnp.sum(grad * normed, axis=0, keepdims=True)], axis=0
    )


def put_totals(totals, held):
    high = totals.astype(BF16).astype(F32)
    rows = jnp.concatenate([high, totals - high], axis=0)
    for tile in range(6):
        held[4 * tile : 4 * tile + 4] = rows[:, 128 * tile : 128 * tile + 128]
    return held[:TOT].astype(BF16)


def get_totals(held):
    rows = jnp.concatenate([held[4 * tile : 4 * tile + 4] for tile in range(6)], axis=1)
    return rows[0:2] + rows[2:4]


def first_kernel(got, message):
    parts = got[...].astype(F32)
    total = jnp.sum(parts, axis=0)
    zero = jnp.zeros((8, 128), F32)
    for l in range(NYL):
        for h in range(NYH):
            tiles = []
            for piece in range(PIECE):
                sub, tile = divmod(l * PIECE + piece, 18)
                row = sub * OWNERS + h * NZ
                tiles.append(total[row : row + 8, 128 * tile : 128 * tile + 128])
            tiles.append(zero)
            message[l * NYH + h] = jnp.concatenate(tiles, axis=0).astype(BF16)


def second_kernel(got, totals, totals_y, message, held, line):
    total = jnp.sum(got[...].astype(F32), axis=0)
    packed = put_totals(totals[...] + totals_y[...], held).astype(F32)
    for piece in range(PIECE):
        line[:, TOT + piece, :] = total[piece * 8 : piece * 8 + 8]
    for z in range(NZ):
        line[z, :TOT] = packed
        line[z, TOT + PIECE :] = jnp.zeros((MSG - TOT - PIECE, 128), F32)
    message[...] = line[...].astype(BF16)


def third_kernel(got, message, held):
    total = jnp.sum(got[...].astype(F32), axis=0)
    held[...] = total[:32]
    packed = put_totals(get_totals(held), held)
    message[...] = spread(jnp.concatenate([packed, total[TOT:].astype(BF16)], axis=0), NX * NYL)


def last_kernel(got, vectors, inputs, cot, pre_grad, grad_in, scaled, held):
    total = jnp.zeros((32, 128), F32)
    for member in range(NX * NYL):
        total += got[member, :32].astype(F32)
    held[...] = total
    totals = get_totals(held)
    scaled[...] = totals * NORM
    rows = vectors[...]
    normed = normalised(inputs[...].astype(F32), rows)
    bn_grad = (rows[2:3] * rows[1:2]) * (
        pre_grad[...] - totals[0:1] / COUNT - normed * (totals[1:2] / COUNT)
    )
    grad_in[...] = (cot[...].astype(F32) + bn_grad).astype(BF16)


def forward_kernel(place, vectors, inputs, mate, outer, own, mine, theirs, channel, output):
    rows = vectors[...]

    def activate(block):
        v = rows[2:3] * normalised(block.astype(F32), rows) + rows[3:4]
        return v * half_gate(v)

    low = place[0] == 0
    here = activate(inputs[...]).astype(BF16)
    near = activate(mate[L:]).astype(BF16)
    away = jnp.where(place[1] == 1, activate(outer[...]), 0.0).astype(BF16)
    taps = (jnp.where(low, away, near), here, jnp.where(low, near, away))
    total = inputs[...].astype(F32)
    pick = one_hot(channel)
    for tap, a in enumerate(taps):
        chosen = jnp.dot(a, pick, preferred_element_type=F32).astype(BF16)
        total += jnp.dot(chosen, by_tap((own, mine, theirs), tap), preferred_element_type=F32)
    output[...] = total.astype(BF16)


def shape(*dims, kind=F32):
    return jax.ShapeDtypeStruct(dims, kind)


def exchange(value, axes):
    return lax.all_to_all(value, axes, 0, 0, tiled=True)


def from_side(value, distance):
    route = []
    for z in range(NZ):
        route.append((((z + distance) % NZ) * NC, z * NC))
        route.append((((z - distance) % NZ) * NC + 1, z * NC + 1))
    return lax.ppermute(value, ("z", "c"), route)


def body(inputs, gain, shift, kernel, cotangent):
    yh, zi, ci = lax.axis_index("yh"), lax.axis_index("z"), lax.axis_index("c")
    inputs, cotangent = inputs[0], cotangent[0]
    gain, shift = gain[None], shift[None]
    seq = (yh * NZ + zi) * NC + ci
    has_outer = jnp.logical_and(seq > 0, seq < SEQ_N - 1).astype(jnp.int32)
    place = jnp.stack([ci, has_outer])
    order = jnp.arange(HALF)
    quarter, row, owner = order // 96, (order // OWNERS) % SUB, order % OWNERS
    source = ((owner * NC + ci) * ROWS + quarter * SUB + row)[None]
    side = 1 - 2 * ci
    ones = [(1, 0), (1, 1), (2, 0), (2, 1), (3, 0), (3, 1)]
    steps = [(zi, 0), (zi, 1)] + [(zi + side * d, p) for d, p in ones] + [(zi + 4, ci)]
    steps += [(zi - side * d, p) for d, p in ones] + [(zi + 4, 1 - ci)]
    base = jnp.stack([(z % NZ) * NC + p for z, p in steps])
    inner = jnp.arange(NYH * ROWS)
    inner = (inner // ROWS) * (NZ * NC * ROWS) + inner % ROWS
    channel = (base[:, None] * ROWS + inner[None]).reshape(1, C)
    swap_c = [(0, 1), (1, 0)]
    swap_out = [(i, j) for i in range(1, SEQ_N - 1, 2) for i, j in ((i, i + 1), (i + 1, i))]
    swap_y = []
    for l in range(NYL):
        for h in range(NYH):
            y = 7 - (h * NYL + l)
            swap_y.append((l * NYH + h, (y % NYL) * NYH + y // NYL))

    stats = call(stats_kernel, shape(NZ * NC, 2, C), "stats", 8)(inputs)
    stats, held_cot, own = lax.optimization_barrier((stats, cotangent, kernel))
    own = own.transpose(1, 0, 2)
    same = lax.ppermute(own, "c", swap_c)
    outer = lax.ppermute(held_cot, SEQ, swap_out)
    low = ci == 0
    own = jnp.stack([jnp.where(low, own, same), jnp.where(low, same, own)])
    other = lax.ppermute(own, ("yl", "yh"), swap_y)
    stats = exchange(stats, ("z", "c"))

    first = yh == 0
    own = jnp.concatenate([jnp.where(first, own, other), jnp.where(first, other, own)], axis=2)
    stats, own, outer, held_in, held_cot = lax.optimization_barrier((stats, own, outer, inputs, cotangent))
    near = from_side(own, 1)
    mate = lax.ppermute(jnp.concatenate([held_cot, held_in], axis=0), "c", swap_c)
    far = lax.ppermute(outer, "c", swap_c)
    stats = call(merge_kernel, shape(NX * NYL * NYH, 2, C), "merge", 8)(stats)
    stats = exchange(stats, ("x", "yl", "yh"))
    stats, near = lax.optimization_barrier((stats, near))
    pair = from_side(jnp.concatenate([own, near], axis=0), 2)

    terms, vectors = call(
        terms_kernel, (shape(HALF, 3 * C, kind=BF16), shape(4, C)), "terms", 24, smem=10,
        flops=2 * 512 * HALF * C * 4, size=6 << 20,
    )(place, stats, gain, shift, source, inputs, mate, cotangent, outer, far)
    terms = exchange(terms.reshape(NX, HALF // NX, 3 * C), "x")

    across = from_side(jnp.where(low, pair[2], pair[3]), 1)
    mine = jnp.concatenate([near, pair, across[None]], axis=0)
    theirs = lax.ppermute(mine, "c", swap_c)
    pre_grad, totals = call(
        back_kernel, (shape(L, C), shape(2, C)), "back", 32, smem=10,
        flops=2 * L * C * C * 5, size=8 << 20,
    )(place, vectors, inputs, mate, cotangent, outer, own, mine, theirs, channel)
    totals = lax.psum(totals, "c")
    totals_y = lax.ppermute(totals, ("yl", "yh"), swap_y)

    held = pltpu.VMEM((32, 128), F32)
    message = call(first_kernel, shape(8, 224, 128, kind=BF16), "first", 12)(terms)
    message, late_in = lax.optimization_barrier((message, inputs))
    outer_in = lax.ppermute(late_in, SEQ, swap_out)
    got = exchange(message, ("yl", "yh"))
    message = call(
        second_kernel, shape(NZ, MSG, 128, kind=BF16), "second", 12,
        scratch=[held, pltpu.VMEM((NZ, MSG, 128), F32)],
    )(got, totals, totals_y)
    got = exchange(message, "z")
    message = call(third_kernel, shape(NX * NYL, MSG, 128, kind=BF16), "third", 12, scratch=[held])(got)
    got = exchange(message, ("x", "yl"))
    output = call(
        forward_kernel, shape(L, C, kind=BF16), "forward", 32, smem=9,
        flops=2 * L * C * C * 6, size=6 << 20,
    )(place, vectors, inputs, mate, outer_in, own, mine, theirs, channel)
    grad_in, scaled = call(
        last_kernel, (shape(L, C, kind=BF16), shape(2, C)), "last", 12, scratch=[held]
    )(got, vectors, inputs, cotangent, pre_grad)
    weight_grad = got[:, TOT : TOT + PIECE].astype(F32).reshape(ROWS, 3, C)
    return (output[None], grad_in[None], weight_grad, scaled[1], scaled[0])


def solution(mesh):
    split_mesh = Mesh(mesh.devices.reshape(NX, NYL, NYH, NZ, NC), AXES)
    rows = P(("x", "yl"), SEQ, None)
    return jax.shard_map(
        body,
        mesh=split_mesh,
        in_specs=(rows, P(), P(), P(SEQ, None, None), rows),
        out_specs=(rows, rows, P(SEQ, None, None), P(), P()),
        check_vma=False,
    )
```

```python
import jax
import jax.numpy as jnp
from jax import lax
from jax.experimental import pallas as pl
from jax.experimental.pallas import tpu as pltpu
from jax.sharding import Mesh, PartitionSpec as P

F32 = jnp.float32
BF16 = jnp.bfloat16
AXES = ("x", "ya", "yb", "yh", "z", "c")
DP = ("x", "ya", "yb")
Y = ("ya", "yb", "yh")
NX, NYA, NYB, NYH, NZ, NC = 4, 2, 2, 2, 8, 2
NYL = NYA * NYB
SEQ = ("yh", "z", "c")
SEQ_N = NYH * NZ * NC
C = 768
HALF = C // 2
L = 256
ROWS = 24
OWNERS = NYH * NZ
SUB = ROWS // (NX * NYB)
PIECE = 27
TOT = 24
MSG = 64
COUNT = L * SEQ_N * NX * NYL
NORM = float(COUNT) ** -0.5
SQRT_HALF = 0.7071067811865476
INV_SQRT_2PI = 0.3989422804014327
NT = (((1,), (1,)), ((), ()))
TN = (((0,), (0,)), ((), ()))
SPACES = {
    "s": pl.BlockSpec(memory_space=pltpu.SMEM),
    "v": pl.BlockSpec(memory_space=pltpu.VMEM),
    "a": pl.BlockSpec(memory_space=pl.ANY),
}


def call(kernel, out_shape, name, megabytes, spaces=None, out_specs=None, flops=0, size=1 << 20, scratch=()):
    params = pltpu.CompilerParams(vmem_limit_bytes=megabytes * 1024 * 1024)
    estimate = pl.CostEstimate(flops=flops, bytes_accessed=size, transcendentals=0)
    extra = {}
    if spaces is not None:
        extra["in_specs"] = [SPACES[letter] for letter in spaces]
    if out_specs is not None:
        extra["out_specs"] = out_specs
    return pl.pallas_call(
        kernel, out_shape=out_shape, compiler_params=params, cost_estimate=estimate, name=name,
        scratch_shapes=list(scratch), **extra,
    )


def fetch(sources, targets, sems):
    copies = [
        pltpu.make_async_copy(source, target, sems.at[i])
        for i, (source, target) in enumerate(zip(sources, targets))
    ]
    for copy in copies:
        copy.start()
    return copies


def spread(value, n):
    return jnp.broadcast_to(value[None], (n,) + value.shape)


def stats_kernel(inputs, message, block, sems):
    fetch([inputs], [block], sems)[0].wait()
    values = block[...].astype(F32)
    total = jnp.sum(values, axis=0, keepdims=True)
    off = values - total / L
    squares = jnp.sum(off * off, axis=0, keepdims=True)
    message[...] = spread(jnp.concatenate([total, squares], axis=0), NZ * NC)


def merged(parts, count):
    sums, squares = parts[:, 0, :], parts[:, 1, :]
    n = sums.shape[0]
    total = jnp.sum(sums, axis=0, keepdims=True)
    off = sums / count - total / (count * n)
    return total, jnp.sum(squares, axis=0, keepdims=True) + count * jnp.sum(off * off, axis=0, keepdims=True)


def merge_kernel(parts, message):
    total, squares = merged(parts[...], L)
    message[...] = spread(jnp.concatenate([total, squares], axis=0), NX * NYL * NYH)


def one_hot(channels):
    rows = lax.broadcasted_iota(jnp.int32, (C, channels.shape[1]), 0)
    return jnp.where(rows == channels[...], 1.0, 0.0).astype(BF16)


def normalised(block, vectors):
    return (block - vectors[0:1]) * vectors[1:2]


def half_gate(v):
    return 0.5 * (1.0 + lax.erf(v * SQRT_HALF))


def terms_kernel(place, parts, gain, shift, source, inputs, mate, cot, outer, terms, vectors):
    total, squares = merged(parts[...], L * NZ * NC)
    mean = total / COUNT
    inv_std = lax.rsqrt(squares / COUNT + 1e-05)
    rows = jnp.concatenate([mean, inv_std, gain[...], shift[...]], axis=0)
    vectors[...] = rows
    pick = one_hot(source)
    chosen, rest = jnp.zeros((4, HALF), F32), rows
    for _ in range(3):
        part = rest.astype(BF16)
        chosen += jnp.dot(part, pick, preferred_element_type=F32)
        rest = rest - part.astype(F32)
    low = place[0] == 0
    both = jnp.concatenate([inputs[...], mate[L : 2 * L]], axis=0)
    v = normalised(jnp.dot(both, pick, preferred_element_type=F32), chosen)
    v = chosen[2:3] * v + chosen[3:4]
    act = (v * half_gate(v)).astype(BF16)
    own, next_own, last_own = cot[...], mate[:L], outer[:L]
    beyond = mate[2 * L :]
    cots = (
        (jnp.where(low, next_own, last_own), jnp.where(low, beyond, own)),
        (own, next_own),
        (jnp.where(low, last_own, next_own), jnp.where(low, own, beyond)),
    )
    for tap, pair in enumerate(cots):
        block = lax.dot_general(act, jnp.concatenate(pair, axis=0), TN, preferred_element_type=F32)
        terms[:, tap * C : (tap + 1) * C] = (block * NORM).astype(BF16)


def by_tap(kern, tap):
    return kern[:, tap].reshape(C, C)


def back_kernel(
    place, vectors, inputs_h, mate_h, cot_h, outer_h, kc, ko, channel, pre_grad, totals,
    inputs, mate, cot, outer, kern, sems,
):
    sources = [inputs_h, mate_h.at[:L], cot_h, outer_h.at[:L], kc, ko]
    copies = fetch(sources, [inputs, mate, cot, outer, kern.at[:NZ], kern.at[NZ:]], sems)
    low = place[0] == 0
    pick = one_hot(channel)
    copies[0].wait()
    rows = vectors[...]
    normed = normalised(inputs[...].astype(F32), rows)
    v = rows[2:3] * normed + rows[3:4]
    slope = half_gate(v) + v * (INV_SQRT_2PI * jnp.exp(-0.5 * v * v))
    for copy in copies[1:]:
        copy.wait()
    taps = (
        jnp.where(low, mate[...], outer[...]),
        cot[...],
        jnp.where(low, outer[...], mate[...]),
    )
    total = jnp.zeros((L, C), F32)
    for tap, q in enumerate(taps):
        total += lax.dot_general(q, by_tap(kern, tap), NT, preferred_element_type=F32)
    high = total.astype(BF16)
    rest = (total - high.astype(F32)).astype(BF16)
    total = lax.dot_general(high, pick, NT, preferred_element_type=F32)
    total += lax.dot_general(rest, pick, NT, preferred_element_type=F32)
    grad = total * slope
    pre_grad[...] = grad
    totals[...] = jnp.concatenate(
        [jnp.sum(grad, axis=0, keepdims=True), jnp.sum(grad * normed, axis=0, keepdims=True)], axis=0
    )


def put_totals(totals, held):
    high = totals.astype(BF16).astype(F32)
    rows = jnp.concatenate([high, totals - high], axis=0)
    for tile in range(6):
        held[4 * tile : 4 * tile + 4] = rows[:, 128 * tile : 128 * tile + 128]
    return held[:TOT].astype(BF16)


def get_totals(held):
    rows = jnp.concatenate([held[4 * tile : 4 * tile + 4] for tile in range(6)], axis=1)
    return rows[0:2] + rows[2:4]


def first_kernel(got, message):
    parts = got[...].astype(F32)
    total = jnp.sum(parts, axis=0)
    zero = jnp.zeros((8, 128), F32)
    for l in range(NYA):
        for h in range(NYH):
            tiles = []
            for piece in range(PIECE):
                sub, tile = divmod(l * PIECE + piece, 18)
                row = sub * OWNERS + h * NZ
                tiles.append(total[row : row + 8, 128 * tile : 128 * tile + 128])
            tiles.append(zero)
            message[l * NYH + h] = jnp.concatenate(tiles, axis=0).astype(BF16)


def second_kernel(got, totals, totals_y, message, held, line):
    total = jnp.sum(got[...].astype(F32), axis=0)
    packed = put_totals(totals[...] + totals_y[...], held).astype(F32)
    for piece in range(PIECE):
        line[:, TOT + piece, :] = total[piece * 8 : piece * 8 + 8]
    for z in range(NZ):
        line[z, :TOT] = packed
        line[z, TOT + PIECE :] = jnp.zeros((MSG - TOT - PIECE, 128), F32)
    message[...] = line[...].astype(BF16)


def third_kernel(got, message, held):
    total = jnp.sum(got[...].astype(F32), axis=0)
    held[...] = total[:32]
    packed = put_totals(get_totals(held), held)
    message[...] = spread(jnp.concatenate([packed, total[TOT:].astype(BF16)], axis=0), NX * NYL)


def last_kernel(
    got, vectors, inputs_h, cot_h, pre_h, grad_in, weights, gain_grad, shift_grad,
    inputs, cot, pre_grad, held, line, sems,
):
    copies = fetch([inputs_h, cot_h, pre_h], [inputs, cot, pre_grad], sems)
    total = jnp.zeros((32, 128), F32)
    for member in range(NX * NYL):
        part = got[member].astype(F32)
        total += part[:32]
        line[...] = part
        x, l = divmod(member, NYL)
        a, b = divmod(l, NYB)
        for piece in range(PIECE):
            sub, tile = divmod(a * PIECE + piece, 18)
            row = (x * NYB + b) * SUB + sub
            tap, lane = divmod(tile, 6)
            weights[tap, row : row + 1, 128 * lane : 128 * lane + 128] = line[TOT + piece : TOT + piece + 1]
    held[...] = total
    totals = get_totals(held)
    shift_grad[...] = (totals[0:1] * NORM).reshape(C)
    gain_grad[...] = (totals[1:2] * NORM).reshape(C)
    for copy in copies:
        copy.wait()
    rows = vectors[...]
    normed = normalised(inputs[...].astype(F32), rows)
    bn_grad = (rows[2:3] * rows[1:2]) * (
        pre_grad[...] - totals[0:1] / COUNT - normed * (totals[1:2] / COUNT)
    )
    grad_in[...] = (cot[...].astype(F32) + bn_grad).astype(BF16)


def acts_kernel(place, vectors, inputs, mate_h, outer_h, channel, acts, mate, outer, sems):
    copies = fetch([outer_h.at[L:], mate_h.at[L : 2 * L]], [outer, mate], sems)
    rows = vectors[...]

    def activate(block):
        v = rows[2:3] * normalised(block.astype(F32), rows) + rows[3:4]
        return v * half_gate(v)

    low = place[0] == 0
    pick = one_hot(channel)
    here = activate(inputs[...]).astype(BF16)
    copies[0].wait()
    away = jnp.where(place[1] == 1, activate(outer[...]), 0.0).astype(BF16)
    copies[1].wait()
    near = activate(mate[...]).astype(BF16)
    for tap, a in enumerate((jnp.where(low, away, near), here, jnp.where(low, near, away))):
        acts[tap] = jnp.dot(a, pick, preferred_element_type=F32).astype(BF16)


def forward_kernel(acts, inputs, kc, ko, output, kern, sems):
    copies = fetch([kc, ko], [kern.at[:NZ], kern.at[NZ:]], sems)
    total = inputs[...].astype(F32)
    for copy in copies:
        copy.wait()
    for tap in range(3):
        total += jnp.dot(acts[tap], by_tap(kern, tap), preferred_element_type=F32)
    output[...] = total.astype(BF16)


def shape(*dims, kind=F32):
    return jax.ShapeDtypeStruct(dims, kind)


def exchange(value, axes):
    return lax.all_to_all(value, axes, 0, 0, tiled=True)


def body(inputs, gain, shift, kernel, cotangent):
    yh, zi, ci = lax.axis_index("yh"), lax.axis_index("z"), lax.axis_index("c")
    inputs, cotangent = inputs[0], cotangent[0]
    gain, shift = gain[None], shift[None]
    seq = (yh * NZ + zi) * NC + ci
    has_outer = jnp.logical_and(seq > 0, seq < SEQ_N - 1).astype(jnp.int32)
    place = jnp.stack([ci, has_outer])
    order = jnp.arange(HALF)
    part, row, owner = order // (SUB * OWNERS), (order // OWNERS) % SUB, order % OWNERS
    source = ((owner * NC + ci) * ROWS + part * SUB + row)[None]
    order = jnp.arange(C)
    gp, gz = order // (NZ * NYH * ROWS), (order // (NYH * ROWS)) % NZ
    gy, gr = (order // ROWS) % NYH, order % ROWS
    channel = ((((gy + yh) % NYH * NZ + gz) * NC + (gp + ci) % NC) * ROWS + gr)[None]
    swap_c = [(0, 1), (1, 0)]
    swap_out = [(i, j) for i in range(1, SEQ_N - 1, 2) for i, j in ((i, i + 1), (i + 1, i))]
    swap_y = []
    for l in range(NYL):
        for h in range(NYH):
            y = 7 - (h * NYL + l)
            swap_y.append((l * NYH + h, (y % NYL) * NYH + y // NYL))

    own = kernel.transpose(1, 0, 2)
    other = lax.ppermute(own, Y, swap_y)
    pair = jnp.concatenate([cotangent, inputs], axis=0)
    stats = call(stats_kernel, shape(NZ * NC, 2, C), "stats", 56, "a", scratch=[
        pltpu.VMEM((L, C), BF16), pltpu.SemaphoreType.DMA((1,)),
    ])(inputs)
    stats, other, pair = lax.optimization_barrier((stats, other, pair))
    outer = lax.ppermute(pair, SEQ, swap_out)
    kernel_c = lax.all_gather(jnp.concatenate([own, other], axis=1), "z", axis=0, tiled=False)
    stats = exchange(stats, ("z", "c"))
    stats, outer, pair = lax.optimization_barrier((stats, outer, pair))
    stats = call(merge_kernel, shape(NX * NYL * NYH, 2, C), "merge", 8)(stats)
    mate = lax.ppermute(jnp.concatenate([pair, outer[:L]], axis=0), "c", swap_c)
    stats = exchange(stats, ("x",) + Y)

    terms, vectors = call(
        terms_kernel, (shape(HALF, 3 * C, kind=BF16), shape(4, C)), "terms", 24, "svvvvvvvv", flops=2 * 512 * HALF * C * 4, size=6 << 20,
    )(place, stats, gain, shift, source, inputs, mate, cotangent, outer)
    terms = exchange(terms.reshape(NX * NYB, HALF // (NX * NYB), 3 * C), ("x", "yb"))

    kernel_o = lax.ppermute(kernel_c, "c", swap_c)
    kern = pltpu.VMEM((2 * NZ, 3, NYH * ROWS, C), BF16)
    pre_grad, totals = call(
        back_kernel, (shape(L, C), shape(2, C)), "back", 56, "svaaaaaav",
        flops=2 * L * C * C * 5, size=8 << 20,
        scratch=[
            pltpu.VMEM((L, C), BF16), pltpu.VMEM((L, C), BF16), pltpu.VMEM((L, C), BF16),
            pltpu.VMEM((L, C), BF16), kern, pltpu.SemaphoreType.DMA((6,)),
        ],
    )(place, vectors, inputs, mate, cotangent, outer, kernel_c, kernel_o, channel)
    totals = lax.psum(totals, "c")

    held = pltpu.VMEM((32, 128), F32)
    terms, totals = lax.optimization_barrier((terms, totals))
    totals_y = lax.ppermute(totals, Y, swap_y)
    message = call(first_kernel, shape(NYA * NYH, 224, 128, kind=BF16), "first", 12)(terms)
    got = exchange(message, ("ya", "yh"))
    message = call(
        second_kernel, shape(NZ, MSG, 128, kind=BF16), "second", 12,
        scratch=[held, pltpu.VMEM((NZ, MSG, 128), F32)],
    )(got, totals, totals_y)
    got = exchange(message, "z")
    acts = call(
        acts_kernel, shape(3, L, C, kind=BF16), "acts", 56, "svvaav", flops=2 * L * C * C * 3, size=2 << 20,
        scratch=[pltpu.VMEM((L, C), BF16), pltpu.VMEM((L, C), BF16), pltpu.SemaphoreType.DMA((2,))],
    )(place, vectors, inputs, mate, outer, channel)
    got, acts = lax.optimization_barrier((got, acts))
    message = call(third_kernel, shape(NX * NYL, MSG, 128, kind=BF16), "third", 12, scratch=[held])(got)
    got = exchange(message, DP)
    output = call(
        forward_kernel, shape(L, C, kind=BF16), "forward", 56, "vvaa", flops=2 * L * C * C * 3, size=6 << 20,
        scratch=[kern, pltpu.SemaphoreType.DMA((2,))],
    )(acts, inputs, kernel_c, kernel_o)
    got, output = lax.optimization_barrier((got, output))
    grad_in, weights, gain_grad, shift_grad = call(
        last_kernel,
        (shape(L, C, kind=BF16), shape(3, ROWS, C), shape(C), shape(C)), "last", 12, "vvaaa",
        scratch=[
            pltpu.VMEM((L, C), BF16), pltpu.VMEM((L, C), BF16), pltpu.VMEM((L, C), F32),
            held, pltpu.VMEM((MSG, 128), F32), pltpu.SemaphoreType.DMA((3,)),
        ],
    )(got, vectors, inputs, cotangent, pre_grad)
    return (output[None], grad_in[None], weights.transpose(1, 0, 2), gain_grad, shift_grad)


def solution(mesh):
    split_mesh = Mesh(mesh.devices.reshape(NX, NYA, NYB, NYH, NZ, NC), AXES)
    rows = P(DP, SEQ, None)
    return jax.shard_map(
        body,
        mesh=split_mesh,
        in_specs=(rows, P(), P(), P(SEQ, None, None), rows),
        out_specs=(rows, rows, P(SEQ, None, None), P(), P()),
        check_vma=False,
    )
```

```python
import jax
import jax.numpy as jnp
from jax import lax
from jax.experimental import pallas as pl
from jax.experimental.pallas import tpu as pltpu
from jax.sharding import Mesh, PartitionSpec as P

F32 = jnp.float32
BF16 = jnp.bfloat16
AXES = ("x", "ya", "yb", "yh", "z", "c")
DP = ("x", "ya", "yb")
Y = ("ya", "yb", "yh")
NX, NYA, NYB, NYH, NZ, NC = 4, 2, 2, 2, 8, 2
NYL = NYA * NYB
SEQ = ("yh", "z", "c")
SEQ_N = NYH * NZ * NC
C = 768
HALF = C // 2
L = 256
ROWS = 24
OWNERS = NYH * NZ
SUB = ROWS // (NX * NYB)
PIECE = 27
TOT = 24
MSG = 64
COUNT = L * SEQ_N * NX * NYL
NORM = float(COUNT) ** -0.5
SQRT_HALF = 0.7071067811865476
INV_SQRT_2PI = 0.3989422804014327
NT = (((1,), (1,)), ((), ()))
TN = (((0,), (0,)), ((), ()))
SPACES = {
    "s": pl.BlockSpec(memory_space=pltpu.SMEM),
    "v": pl.BlockSpec(memory_space=pltpu.VMEM),
    "a": pl.BlockSpec(memory_space=pl.ANY),
}


def call(kernel, out_shape, name, megabytes, spaces=None, out_specs=None, flops=0, size=1 << 20, scratch=()):
    params = pltpu.CompilerParams(vmem_limit_bytes=megabytes * 1024 * 1024)
    estimate = pl.CostEstimate(flops=flops, bytes_accessed=size, transcendentals=0)
    extra = {}
    if spaces is not None:
        extra["in_specs"] = [SPACES[letter] for letter in spaces]
    if out_specs is not None:
        extra["out_specs"] = out_specs
    return pl.pallas_call(
        kernel, out_shape=out_shape, compiler_params=params, cost_estimate=estimate, name=name,
        scratch_shapes=list(scratch), **extra,
    )


def fetch(sources, targets, sems):
    copies = [
        pltpu.make_async_copy(source, target, sems.at[i])
        for i, (source, target) in enumerate(zip(sources, targets))
    ]
    for copy in copies:
        copy.start()
    return copies


def spread(value, n):
    return jnp.broadcast_to(value[None], (n,) + value.shape)


def stats_kernel(inputs, message, block, sems):
    fetch([inputs], [block], sems)[0].wait()
    values = block[...].astype(F32)
    total = jnp.sum(values, axis=0, keepdims=True)
    off = values - total / L
    squares = jnp.sum(off * off, axis=0, keepdims=True)
    message[...] = spread(jnp.concatenate([total, squares], axis=0), NZ * NC)


def merged(parts, count):
    sums, squares = parts[:, 0, :], parts[:, 1, :]
    n = sums.shape[0]
    total = jnp.sum(sums, axis=0, keepdims=True)
    off = sums / count - total / (count * n)
    return total, jnp.sum(squares, axis=0, keepdims=True) + count * jnp.sum(off * off, axis=0, keepdims=True)


def merge_kernel(parts, message):
    total, squares = merged(parts[...], L)
    message[...] = spread(jnp.concatenate([total, squares], axis=0), NX * NYL * NYH)


def one_hot(channels):
    rows = lax.broadcasted_iota(jnp.int32, (C, channels.shape[1]), 0)
    return jnp.where(rows == channels[...], 1.0, 0.0).astype(BF16)


def normalised(block, vectors):
    return (block - vectors[0:1]) * vectors[1:2]


def half_gate(v):
    return 0.5 * (1.0 + lax.erf(v * SQRT_HALF))


def terms_kernel(place, parts, gain, shift, source, inputs, mate, cot, outer, terms, vectors):
    total, squares = merged(parts[...], L * NZ * NC)
    mean = total / COUNT
    inv_std = lax.rsqrt(squares / COUNT + 1e-05)
    rows = jnp.concatenate([mean, inv_std, gain[...], shift[...]], axis=0)
    vectors[...] = rows
    pick = one_hot(source)
    chosen, rest = jnp.zeros((4, HALF), F32), rows
    for _ in range(3):
        part = rest.astype(BF16)
        chosen += jnp.dot(part, pick, preferred_element_type=F32)
        rest = rest - part.astype(F32)
    low = place[0] == 0
    both = jnp.concatenate([inputs[...], mate[L : 2 * L]], axis=0)
    v = normalised(jnp.dot(both, pick, preferred_element_type=F32), chosen)
    v = chosen[2:3] * v + chosen[3:4]
    act = (v * half_gate(v)).astype(BF16)
    own, next_own, last_own = cot[...], mate[:L], outer[...]
    beyond = mate[2 * L :]
    cots = (
        (jnp.where(low, next_own, last_own), jnp.where(low, beyond, own)),
        (own, next_own),
        (jnp.where(low, last_own, next_own), jnp.where(low, own, beyond)),
    )
    for tap, pair in enumerate(cots):
        block = lax.dot_general(act, jnp.concatenate(pair, axis=0), TN, preferred_element_type=F32)
        terms[:, tap * C : (tap + 1) * C] = (block * NORM).astype(BF16)


def by_tap(kern, tap):
    return kern[:, tap].reshape(C, C)


def back_kernel(
    place, vectors, inputs_h, mate_h, cot_h, outer_h, kc, ko, channel, pre_grad, totals,
    inputs, mate, cot, outer, kern, sems,
):
    sources = [inputs_h, mate_h.at[:L], cot_h, outer_h, kc, ko]
    copies = fetch(sources, [inputs, mate, cot, outer, kern.at[:NZ], kern.at[NZ:]], sems)
    low = place[0] == 0
    pick = one_hot(channel)
    copies[0].wait()
    rows = vectors[...]
    normed = normalised(inputs[...].astype(F32), rows)
    v = rows[2:3] * normed + rows[3:4]
    slope = half_gate(v) + v * (INV_SQRT_2PI * jnp.exp(-0.5 * v * v))
    for copy in copies[1:]:
        copy.wait()
    taps = (
        jnp.where(low, mate[...], outer[...]),
        cot[...],
        jnp.where(low, outer[...], mate[...]),
    )
    total = jnp.zeros((L, C), F32)
    for tap, q in enumerate(taps):
        total += lax.dot_general(q, by_tap(kern, tap), NT, preferred_element_type=F32)
    high = total.astype(BF16)
    rest = (total - high.astype(F32)).astype(BF16)
    total = lax.dot_general(high, pick, NT, preferred_element_type=F32)
    total += lax.dot_general(rest, pick, NT, preferred_element_type=F32)
    grad = total * slope
    pre_grad[...] = grad
    totals[...] = jnp.concatenate(
        [jnp.sum(grad, axis=0, keepdims=True), jnp.sum(grad * normed, axis=0, keepdims=True)], axis=0
    )


def put_totals(totals, held):
    high = totals.astype(BF16).astype(F32)
    rows = jnp.concatenate([high, totals - high], axis=0)
    for tile in range(6):
        held[4 * tile : 4 * tile + 4] = rows[:, 128 * tile : 128 * tile + 128]
    return held[:TOT].astype(BF16)


def get_totals(held):
    rows = jnp.concatenate([held[4 * tile : 4 * tile + 4] for tile in range(6)], axis=1)
    return rows[0:2] + rows[2:4]


def first_kernel(got, totals, message, held):
    packed = put_totals(totals[...], held).astype(F32)
    parts = got[...].astype(F32)
    total = jnp.sum(parts, axis=0)
    zero = jnp.zeros((8, 128), F32)
    for l in range(NYA):
        for h in range(NYH):
            tiles = []
            for piece in range(PIECE):
                sub, tile = divmod(l * PIECE + piece, 18)
                row = sub * OWNERS + h * NZ
                tiles.append(total[row : row + 8, 128 * tile : 128 * tile + 128])
            tiles += [packed, zero, zero]
            message[l * NYH + h] = jnp.concatenate(tiles, axis=0).astype(BF16)


def second_kernel(got, message, held, line):
    total = jnp.sum(got[...].astype(F32), axis=0)
    held[...] = total[PIECE * 8 : PIECE * 8 + 32]
    packed = put_totals(get_totals(held), held).astype(F32)
    for piece in range(PIECE):
        line[:, TOT + piece, :] = total[piece * 8 : piece * 8 + 8]
    for z in range(NZ):
        line[z, :TOT] = packed
        line[z, TOT + PIECE :] = jnp.zeros((MSG - TOT - PIECE, 128), F32)
    message[...] = line[...].astype(BF16)


def third_kernel(got, message, held):
    total = jnp.sum(got[...].astype(F32), axis=0)
    held[...] = total[:32]
    packed = put_totals(get_totals(held), held)
    message[...] = spread(jnp.concatenate([packed, total[TOT:].astype(BF16)], axis=0), NX * NYL)


def last_kernel(
    got, vectors, inputs_h, cot_h, pre_h, grad_in, weights, gain_grad, shift_grad,
    inputs, cot, pre_grad, held, line, sems,
):
    copies = fetch([inputs_h, cot_h, pre_h], [inputs, cot, pre_grad], sems)
    total = jnp.zeros((32, 128), F32)
    for member in range(NX * NYL):
        part = got[member].astype(F32)
        line[...] = part
        x, l = divmod(member, NYL)
        a, b = divmod(l, NYB)
        if a == 0:
            total += part[:32]
        for piece in range(PIECE):
            sub, tile = divmod(a * PIECE + piece, 18)
            row = (x * NYB + b) * SUB + sub
            tap, lane = divmod(tile, 6)
            weights[tap, row : row + 1, 128 * lane : 128 * lane + 128] = line[TOT + piece : TOT + piece + 1]
    held[...] = total
    totals = get_totals(held)
    shift_grad[...] = (totals[0:1] * NORM).reshape(C)
    gain_grad[...] = (totals[1:2] * NORM).reshape(C)
    for copy in copies:
        copy.wait()
    rows = vectors[...]
    normed = normalised(inputs[...].astype(F32), rows)
    bn_grad = (rows[2:3] * rows[1:2]) * (
        pre_grad[...] - totals[0:1] / COUNT - normed * (totals[1:2] / COUNT)
    )
    grad_in[...] = (cot[...].astype(F32) + bn_grad).astype(BF16)


def activated(block, rows):
    v = rows[2:3] * normalised(block.astype(F32), rows) + rows[3:4]
    return v * half_gate(v)


def acts_kernel(vectors, inputs, mate_h, channel, acts, mate, sems):
    copies = fetch([mate_h.at[L : 2 * L]], [mate], sems)
    rows = vectors[...]
    pick = one_hot(channel)
    here = activated(inputs[...], rows).astype(BF16)
    acts[0] = jnp.dot(here, pick, preferred_element_type=F32).astype(BF16)
    copies[0].wait()
    near = activated(mate[...], rows).astype(BF16)
    acts[1] = jnp.dot(near, pick, preferred_element_type=F32).astype(BF16)


def forward_kernel(place, vectors, acts, inputs, outer, channel, kc, ko, output, kern, sems):
    copies = fetch([kc, ko], [kern.at[:NZ], kern.at[NZ:]], sems)
    low = place[0] == 0
    away = jnp.where(place[1] == 1, activated(outer[...], vectors[...]), 0.0).astype(BF16)
    away = jnp.dot(away, one_hot(channel), preferred_element_type=F32).astype(BF16)
    near = acts[1]
    total = inputs[...].astype(F32)
    for copy in copies:
        copy.wait()
    for tap, a in enumerate((jnp.where(low, away, near), acts[0], jnp.where(low, near, away))):
        total += jnp.dot(a, by_tap(kern, tap), preferred_element_type=F32)
    output[...] = total.astype(BF16)


def shape(*dims, kind=F32):
    return jax.ShapeDtypeStruct(dims, kind)


def exchange(value, axes):
    return lax.all_to_all(value, axes, 0, 0, tiled=True)


def body(inputs, gain, shift, kernel, cotangent):
    yh, zi, ci = lax.axis_index("yh"), lax.axis_index("z"), lax.axis_index("c")
    inputs, cotangent = inputs[0], cotangent[0]
    gain, shift = gain[None], shift[None]
    seq = (yh * NZ + zi) * NC + ci
    has_outer = jnp.logical_and(seq > 0, seq < SEQ_N - 1).astype(jnp.int32)
    place = jnp.stack([ci, has_outer])
    order = jnp.arange(HALF)
    part, row, owner = order // (SUB * OWNERS), (order // OWNERS) % SUB, order % OWNERS
    source = ((owner * NC + ci) * ROWS + part * SUB + row)[None]
    order = jnp.arange(C)
    gp, gz = order // (NZ * NYH * ROWS), (order // (NYH * ROWS)) % NZ
    gy, gr = (order // ROWS) % NYH, order % ROWS
    channel = ((((gy + yh) % NYH * NZ + gz) * NC + (gp + ci) % NC) * ROWS + gr)[None]
    swap_c = [(0, 1), (1, 0)]
    swap_out = [(i, j) for i in range(1, SEQ_N - 1, 2) for i, j in ((i, i + 1), (i + 1, i))]
    swap_y = []
    for l in range(NYL):
        for h in range(NYH):
            y = 7 - (h * NYL + l)
            swap_y.append((l * NYH + h, (y % NYL) * NYH + y // NYL))

    own = kernel.transpose(1, 0, 2)
    other = lax.ppermute(own, Y, swap_y)
    stats = call(stats_kernel, shape(NZ * NC, 2, C), "stats", 8, "a", scratch=[
        pltpu.VMEM((L, C), BF16), pltpu.SemaphoreType.DMA((1,)),
    ])(inputs)
    stats, other, held_cot = lax.optimization_barrier((stats, other, cotangent))
    outer = lax.ppermute(held_cot, SEQ, swap_out)
    kernel_c = lax.all_gather(jnp.concatenate([own, other], axis=1), "z", axis=0, tiled=False)
    stats = exchange(stats, ("z", "c"))
    stats, outer, held_cot, held_in = lax.optimization_barrier((stats, outer, cotangent, inputs))
    stats = call(merge_kernel, shape(NX * NYL * NYH, 2, C), "merge", 8)(stats)
    mate = lax.ppermute(jnp.concatenate([held_cot, held_in, outer], axis=0), "c", swap_c)
    stats = exchange(stats, ("x",) + Y)

    terms, vectors = call(
        terms_kernel, (shape(HALF, 3 * C, kind=BF16), shape(4, C)), "terms", 24, "svvvvvvvv", flops=2 * 512 * HALF * C * 4, size=6 << 20,
    )(place, stats, gain, shift, source, inputs, mate, cotangent, outer)
    terms = exchange(terms.reshape(NX * NYB, HALF // (NX * NYB), 3 * C), ("x", "yb"))

    kernel_o = lax.ppermute(kernel_c, "c", swap_c)
    kern = pltpu.VMEM((2 * NZ, 3, NYH * ROWS, C), BF16)
    pre_grad, totals = call(
        back_kernel, (shape(L, C), shape(2, C)), "back", 56, "svaaaaaav",
        flops=2 * L * C * C * 5, size=8 << 20,
        scratch=[
            pltpu.VMEM((L, C), BF16), pltpu.VMEM((L, C), BF16), pltpu.VMEM((L, C), BF16),
            pltpu.VMEM((L, C), BF16), kern, pltpu.SemaphoreType.DMA((6,)),
        ],
    )(place, vectors, inputs, mate, cotangent, outer, kernel_c, kernel_o, channel)
    totals = lax.psum(totals, "c")

    held = pltpu.VMEM((32, 128), F32)
    message = call(
        first_kernel, shape(NYA * NYH, 256, 128, kind=BF16), "first", 12, scratch=[held]
    )(terms, totals)
    got = exchange(message, ("ya", "yh"))
    message = call(
        second_kernel, shape(NZ, MSG, 128, kind=BF16), "second", 12,
        scratch=[held, pltpu.VMEM((NZ, MSG, 128), F32)],
    )(got)
    message, late_in = lax.optimization_barrier((message, inputs))
    outer_in = lax.ppermute(late_in, SEQ, swap_out)
    got = exchange(message, "z")
    acts = call(
        acts_kernel, shape(2, L, C, kind=BF16), "acts", 56, "vvav", flops=2 * L * C * C * 2, size=2 << 20,
        scratch=[pltpu.VMEM((L, C), BF16), pltpu.SemaphoreType.DMA((1,))],
    )(vectors, inputs, mate, channel)
    got, acts = lax.optimization_barrier((got, acts))
    message = call(third_kernel, shape(NX * NYL, MSG, 128, kind=BF16), "third", 12, scratch=[held])(got)
    got = exchange(message, DP)
    output = call(
        forward_kernel, shape(L, C, kind=BF16), "forward", 56, "svvvvvaa", flops=2 * L * C * C * 4, size=6 << 20,
        scratch=[kern, pltpu.SemaphoreType.DMA((2,))],
    )(place, vectors, acts, inputs, outer_in, channel, kernel_c, kernel_o)
    got, output = lax.optimization_barrier((got, output))
    grad_in, weights, gain_grad, shift_grad = call(
        last_kernel,
        (shape(L, C, kind=BF16), shape(3, ROWS, C), shape(C), shape(C)), "last", 12, "vvaaa",
        scratch=[
            pltpu.VMEM((L, C), BF16), pltpu.VMEM((L, C), BF16), pltpu.VMEM((L, C), F32),
            held, pltpu.VMEM((MSG, 128), F32), pltpu.SemaphoreType.DMA((3,)),
        ],
    )(got, vectors, inputs, cotangent, pre_grad)
    return (output[None], grad_in[None], weights.transpose(1, 0, 2), gain_grad, shift_grad)


def solution(mesh):
    split_mesh = Mesh(mesh.devices.reshape(NX, NYA, NYB, NYH, NZ, NC), AXES)
    rows = P(DP, SEQ, None)
    return jax.shard_map(
        body,
        mesh=split_mesh,
        in_specs=(rows, P(), P(), P(SEQ, None, None), rows),
        out_specs=(rows, rows, P(SEQ, None, None), P(), P()),
        check_vma=False,
    )
```

```python
import jax
import jax.numpy as jnp
from jax import lax
from jax.experimental import pallas as pl
from jax.experimental.pallas import tpu as pltpu
from jax.sharding import Mesh, PartitionSpec as P

F32 = jnp.float32
BF16 = jnp.bfloat16
AXES = ("x", "ya", "yb", "yh", "z", "c")
DP = ("x", "ya", "yb")
Y = ("ya", "yb", "yh")
NX, NYA, NYB, NYH, NZ, NC = 4, 2, 2, 2, 8, 2
NYL = NYA * NYB
SEQ = ("yh", "z", "c")
SEQ_N = NYH * NZ * NC
C = 768
HALF = C // 2
L = 256
ROWS = 24
OWNERS = NYH * NZ
SUB = ROWS // (NX * NYB)
PIECE = 27
TOT = 24
MSG = 64
COUNT = L * SEQ_N * NX * NYL
NORM = float(COUNT) ** -0.5
SQRT_HALF = 0.7071067811865476
INV_SQRT_2PI = 0.3989422804014327
NT = (((1,), (1,)), ((), ()))
TN = (((0,), (0,)), ((), ()))
SPACES = {
    "s": pl.BlockSpec(memory_space=pltpu.SMEM),
    "v": pl.BlockSpec(memory_space=pltpu.VMEM),
    "a": pl.BlockSpec(memory_space=pl.ANY),
}


def call(kernel, out_shape, name, megabytes, spaces=None, out_specs=None, flops=0, size=1 << 20, scratch=()):
    params = pltpu.CompilerParams(vmem_limit_bytes=megabytes * 1024 * 1024)
    estimate = pl.CostEstimate(flops=flops, bytes_accessed=size, transcendentals=0)
    extra = {}
    if spaces is not None:
        extra["in_specs"] = [SPACES[letter] for letter in spaces]
    if out_specs is not None:
        extra["out_specs"] = out_specs
    return pl.pallas_call(
        kernel, out_shape=out_shape, compiler_params=params, cost_estimate=estimate, name=name,
        scratch_shapes=list(scratch), **extra,
    )


def fetch(sources, targets, sems):
    copies = [
        pltpu.make_async_copy(source, target, sems.at[i])
        for i, (source, target) in enumerate(zip(sources, targets))
    ]
    for copy in copies:
        copy.start()
    return copies


def spread(value, n):
    return jnp.broadcast_to(value[None], (n,) + value.shape)


def stats_kernel(inputs, message, block, sems):
    fetch([inputs], [block], sems)[0].wait()
    values = block[...].astype(F32)
    total = jnp.sum(values, axis=0, keepdims=True)
    off = values - total / L
    squares = jnp.sum(off * off, axis=0, keepdims=True)
    message[...] = spread(jnp.concatenate([total, squares], axis=0), NZ * NC)


def merged(parts, count):
    sums, squares = parts[:, 0, :], parts[:, 1, :]
    n = sums.shape[0]
    total = jnp.sum(sums, axis=0, keepdims=True)
    off = sums / count - total / (count * n)
    return total, jnp.sum(squares, axis=0, keepdims=True) + count * jnp.sum(off * off, axis=0, keepdims=True)


def merge_kernel(parts, message):
    total, squares = merged(parts[...], L)
    message[...] = spread(jnp.concatenate([total, squares], axis=0), NX * NYL * NYH)


def one_hot(channels):
    rows = lax.broadcasted_iota(jnp.int32, (C, channels.shape[1]), 0)
    return jnp.where(rows == channels[...], 1.0, 0.0).astype(BF16)


def normalised(block, vectors):
    return (block - vectors[0:1]) * vectors[1:2]


def half_gate(v):
    return 0.5 * (1.0 + lax.erf(v * SQRT_HALF))


def prepare_kernel(parts, gain, shift, source, inputs, vectors, chosen, act):
    total, squares = merged(parts[...], L * NZ * NC)
    mean = total / COUNT
    inv_std = lax.rsqrt(squares / COUNT + 1e-05)
    rows = jnp.concatenate([mean, inv_std, gain[...], shift[...]], axis=0)
    vectors[...] = rows
    pick = one_hot(source)
    some, rest = jnp.zeros((4, HALF), F32), rows
    for _ in range(3):
        part = rest.astype(BF16)
        some += jnp.dot(part, pick, preferred_element_type=F32)
        rest = rest - part.astype(F32)
    chosen[...] = some
    act[...] = activated(jnp.dot(inputs[...], pick, preferred_element_type=F32), some).astype(BF16)


def terms_kernel(place, chosen, act_own, source, mate, cot, outer, terms):
    low = place[0] == 0
    near = jnp.dot(mate[L : 2 * L], one_hot(source), preferred_element_type=F32)
    act = jnp.concatenate([act_own[...], activated(near, chosen[...]).astype(BF16)], axis=0)
    own, next_own, last_own = cot[...], mate[:L], outer[...]
    beyond = mate[2 * L :]
    cots = (
        (jnp.where(low, next_own, last_own), jnp.where(low, beyond, own)),
        (own, next_own),
        (jnp.where(low, last_own, next_own), jnp.where(low, own, beyond)),
    )
    for tap, pair in enumerate(cots):
        block = lax.dot_general(act, jnp.concatenate(pair, axis=0), TN, preferred_element_type=F32)
        terms[:, tap * C : (tap + 1) * C] = (block * NORM).astype(BF16)


def by_tap(kern, tap):
    return kern[:, tap].reshape(C, C)


def back_kernel(
    place, vectors, inputs_h, mate_h, cot_h, outer_h, kc, ko, channel, pre_grad, totals,
    inputs, mate, cot, outer, kern, sems,
):
    sources = [inputs_h, mate_h.at[:L], cot_h, outer_h, kc, ko]
    copies = fetch(sources, [inputs, mate, cot, outer, kern.at[:NZ], kern.at[NZ:]], sems)
    low = place[0] == 0
    pick = one_hot(channel)
    copies[0].wait()
    rows = vectors[...]
    normed = normalised(inputs[...].astype(F32), rows)
    v = rows[2:3] * normed + rows[3:4]
    slope = half_gate(v) + v * (INV_SQRT_2PI * jnp.exp(-0.5 * v * v))
    for copy in copies[1:]:
        copy.wait()
    taps = (
        jnp.where(low, mate[...], outer[...]),
        cot[...],
        jnp.where(low, outer[...], mate[...]),
    )
    total = jnp.zeros((L, C), F32)
    for tap, q in enumerate(taps):
        total += lax.dot_general(q, by_tap(kern, tap), NT, preferred_element_type=F32)
    high = total.astype(BF16)
    rest = (total - high.astype(F32)).astype(BF16)
    total = lax.dot_general(high, pick, NT, preferred_element_type=F32)
    total += lax.dot_general(rest, pick, NT, preferred_element_type=F32)
    grad = total * slope
    pre_grad[...] = grad
    totals[...] = jnp.concatenate(
        [jnp.sum(grad, axis=0, keepdims=True), jnp.sum(grad * normed, axis=0, keepdims=True)], axis=0
    )


def put_totals(totals, held):
    high = totals.astype(BF16).astype(F32)
    rows = jnp.concatenate([high, totals - high], axis=0)
    for tile in range(6):
        held[4 * tile : 4 * tile + 4] = rows[:, 128 * tile : 128 * tile + 128]
    return held[:TOT].astype(BF16)


def get_totals(held):
    rows = jnp.concatenate([held[4 * tile : 4 * tile + 4] for tile in range(6)], axis=1)
    return rows[0:2] + rows[2:4]


def first_kernel(got, totals, message, held):
    packed = put_totals(totals[...], held).astype(F32)
    parts = got[...].astype(F32)
    total = jnp.sum(parts, axis=0)
    zero = jnp.zeros((8, 128), F32)
    for l in range(NYA):
        for h in range(NYH):
            tiles = []
            for piece in range(PIECE):
                sub, tile = divmod(l * PIECE + piece, 18)
                row = sub * OWNERS + h * NZ
                tiles.append(total[row : row + 8, 128 * tile : 128 * tile + 128])
            tiles += [packed, zero, zero]
            message[l * NYH + h] = jnp.concatenate(tiles, axis=0).astype(BF16)


def second_kernel(got, message, held, line):
    total = jnp.sum(got[...].astype(F32), axis=0)
    held[...] = total[PIECE * 8 : PIECE * 8 + 32]
    packed = put_totals(get_totals(held), held).astype(F32)
    for piece in range(PIECE):
        line[:, TOT + piece, :] = total[piece * 8 : piece * 8 + 8]
    for z in range(NZ):
        line[z, :TOT] = packed
        line[z, TOT + PIECE :] = jnp.zeros((MSG - TOT - PIECE, 128), F32)
    message[...] = line[...].astype(BF16)


def third_kernel(got, message, held):
    total = jnp.sum(got[...].astype(F32), axis=0)
    held[...] = total[:32]
    packed = put_totals(get_totals(held), held)
    message[...] = spread(jnp.concatenate([packed, total[TOT:].astype(BF16)], axis=0), NX * NYL)


def last_kernel(
    got, vectors, inputs_h, cot_h, pre_h, grad_in, weights, gain_grad, shift_grad,
    inputs, cot, pre_grad, held, line, sems,
):
    copies = fetch([inputs_h, cot_h, pre_h], [inputs, cot, pre_grad], sems)
    total = jnp.zeros((32, 128), F32)
    for member in range(NX * NYL):
        part = got[member].astype(F32)
        line[...] = part
        x, l = divmod(member, NYL)
        a, b = divmod(l, NYB)
        if a == 0:
            total += part[:32]
        for piece in range(PIECE):
            sub, tile = divmod(a * PIECE + piece, 18)
            row = (x * NYB + b) * SUB + sub
            tap, lane = divmod(tile, 6)
            weights[tap, row : row + 1, 128 * lane : 128 * lane + 128] = line[TOT + piece : TOT + piece + 1]
    held[...] = total
    totals = get_totals(held)
    shift_grad[...] = (totals[0:1] * NORM).reshape(C)
    gain_grad[...] = (totals[1:2] * NORM).reshape(C)
    for copy in copies:
        copy.wait()
    rows = vectors[...]
    normed = normalised(inputs[...].astype(F32), rows)
    bn_grad = (rows[2:3] * rows[1:2]) * (
        pre_grad[...] - totals[0:1] / COUNT - normed * (totals[1:2] / COUNT)
    )
    grad_in[...] = (cot[...].astype(F32) + bn_grad).astype(BF16)


def activated(block, rows):
    v = rows[2:3] * normalised(block.astype(F32), rows) + rows[3:4]
    return v * half_gate(v)


def acts_kernel(place, vectors, inputs, mate_h, outer, channel, acts, mate, sems):
    copies = fetch([mate_h.at[L : 2 * L]], [mate], sems)
    rows = vectors[...]
    pick = one_hot(channel)
    low = place[0] == 0
    here = activated(inputs[...], rows).astype(BF16)
    away = jnp.where(place[1] == 1, activated(outer[...], rows), 0.0).astype(BF16)
    copies[0].wait()
    near = activated(mate[...], rows).astype(BF16)
    for tap, a in enumerate((jnp.where(low, away, near), here, jnp.where(low, near, away))):
        acts[tap] = jnp.dot(a, pick, preferred_element_type=F32).astype(BF16)


def forward_kernel(acts, inputs, kc, ko, output, kern, sems):
    copies = fetch([kc, ko], [kern.at[:NZ], kern.at[NZ:]], sems)
    total = inputs[...].astype(F32)
    for copy in copies:
        copy.wait()
    for tap in range(3):
        total += jnp.dot(acts[tap], by_tap(kern, tap), preferred_element_type=F32)
    output[...] = total.astype(BF16)


def shape(*dims, kind=F32):
    return jax.ShapeDtypeStruct(dims, kind)


def exchange(value, axes):
    return lax.all_to_all(value, axes, 0, 0, tiled=True)


def body(inputs, gain, shift, kernel, cotangent):
    yh, zi, ci = lax.axis_index("yh"), lax.axis_index("z"), lax.axis_index("c")
    inputs, cotangent = inputs[0], cotangent[0]
    gain, shift = gain[None], shift[None]
    seq = (yh * NZ + zi) * NC + ci
    has_outer = jnp.logical_and(seq > 0, seq < SEQ_N - 1).astype(jnp.int32)
    place = jnp.stack([ci, has_outer])
    order = jnp.arange(HALF)
    part, row, owner = order // (SUB * OWNERS), (order // OWNERS) % SUB, order % OWNERS
    source = ((owner * NC + ci) * ROWS + part * SUB + row)[None]
    order = jnp.arange(C)
    gp, gz = order // (NZ * NYH * ROWS), (order // (NYH * ROWS)) % NZ
    gy, gr = (order // ROWS) % NYH, order % ROWS
    channel = ((((gy + yh) % NYH * NZ + gz) * NC + (gp + ci) % NC) * ROWS + gr)[None]
    swap_c = [(0, 1), (1, 0)]
    swap_out = [(i, j) for i in range(1, SEQ_N - 1, 2) for i, j in ((i, i + 1), (i + 1, i))]
    swap_y = []
    for l in range(NYL):
        for h in range(NYH):
            y = 7 - (h * NYL + l)
            swap_y.append((l * NYH + h, (y % NYL) * NYH + y // NYL))

    own = kernel.transpose(1, 0, 2)
    other = lax.ppermute(own, Y, swap_y)
    stats = call(stats_kernel, shape(NZ * NC, 2, C), "stats", 8, "a", scratch=[
        pltpu.VMEM((L, C), BF16), pltpu.SemaphoreType.DMA((1,)),
    ])(inputs)
    stats, other, held_cot = lax.optimization_barrier((stats, other, cotangent))
    outer = lax.ppermute(held_cot, SEQ, swap_out)
    kernel_c = lax.all_gather(jnp.concatenate([own, other], axis=1), "z", axis=0, tiled=False)
    stats = exchange(stats, ("z", "c"))
    stats, outer, held_cot, held_in = lax.optimization_barrier((stats, outer, cotangent, inputs))
    stats = call(merge_kernel, shape(NX * NYL * NYH, 2, C), "merge", 8)(stats)
    mate = lax.ppermute(jnp.concatenate([held_cot, held_in, outer], axis=0), "c", swap_c)
    stats = exchange(stats, ("x",) + Y)

    vectors, chosen, act_own = call(
        prepare_kernel, (shape(4, C), shape(4, HALF), shape(L, HALF, kind=BF16)), "prepare", 24,
    )(stats, gain, shift, source, inputs)
    terms = call(
        terms_kernel, shape(HALF, 3 * C, kind=BF16), "terms", 24, "svvvvvv",
        flops=2 * 512 * HALF * C * 4, size=6 << 20,
    )(place, chosen, act_own, source, mate, cotangent, outer)
    terms = exchange(terms.reshape(NX * NYB, HALF // (NX * NYB), 3 * C), ("x", "yb"))

    kernel_o = lax.ppermute(kernel_c, "c", swap_c)
    kern = pltpu.VMEM((2 * NZ, 3, NYH * ROWS, C), BF16)
    pre_grad, totals = call(
        back_kernel, (shape(L, C), shape(2, C)), "back", 56, "svaaaaaav",
        flops=2 * L * C * C * 5, size=8 << 20,
        scratch=[
            pltpu.VMEM((L, C), BF16), pltpu.VMEM((L, C), BF16), pltpu.VMEM((L, C), BF16),
            pltpu.VMEM((L, C), BF16), kern, pltpu.SemaphoreType.DMA((6,)),
        ],
    )(place, vectors, inputs, mate, cotangent, outer, kernel_c, kernel_o, channel)
    totals = lax.psum(totals, "c")

    held = pltpu.VMEM((32, 128), F32)
    message = call(
        first_kernel, shape(NYA * NYH, 256, 128, kind=BF16), "first", 12, scratch=[held]
    )(terms, totals)
    message, late_in = lax.optimization_barrier((message, inputs))
    outer_in = lax.ppermute(late_in, SEQ, swap_out)
    got = exchange(message, ("ya", "yh"))
    message = call(
        second_kernel, shape(NZ, MSG, 128, kind=BF16), "second", 12,
        scratch=[held, pltpu.VMEM((NZ, MSG, 128), F32)],
    )(got)
    got = exchange(message, "z")
    acts = call(
        acts_kernel, shape(3, L, C, kind=BF16), "acts", 56, "svvavv", flops=2 * L * C * C * 3, size=2 << 20,
        scratch=[pltpu.VMEM((L, C), BF16), pltpu.SemaphoreType.DMA((1,))],
    )(place, vectors, inputs, mate, outer_in, channel)
    got, acts = lax.optimization_barrier((got, acts))
    message = call(third_kernel, shape(NX * NYL, MSG, 128, kind=BF16), "third", 12, scratch=[held])(got)
    got = exchange(message, DP)
    output = call(
        forward_kernel, shape(L, C, kind=BF16), "forward", 56, "vvaa", flops=2 * L * C * C * 3, size=6 << 20,
        scratch=[kern, pltpu.SemaphoreType.DMA((2,))],
    )(acts, inputs, kernel_c, kernel_o)
    got, output = lax.optimization_barrier((got, output))
    grad_in, weights, gain_grad, shift_grad = call(
        last_kernel,
        (shape(L, C, kind=BF16), shape(3, ROWS, C), shape(C), shape(C)), "last", 12, "vvaaa",
        scratch=[
            pltpu.VMEM((L, C), BF16), pltpu.VMEM((L, C), BF16), pltpu.VMEM((L, C), F32),
            held, pltpu.VMEM((MSG, 128), F32), pltpu.SemaphoreType.DMA((3,)),
        ],
    )(got, vectors, inputs, cotangent, pre_grad)
    return (output[None], grad_in[None], weights.transpose(1, 0, 2), gain_grad, shift_grad)


def solution(mesh):
    split_mesh = Mesh(mesh.devices.reshape(NX, NYA, NYB, NYH, NZ, NC), AXES)
    rows = P(DP, SEQ, None)
    return jax.shard_map(
        body,
        mesh=split_mesh,
        in_specs=(rows, P(), P(), P(SEQ, None, None), rows),
        out_specs=(rows, rows, P(SEQ, None, None), P(), P()),
        check_vma=False,
    )
```

```python
import jax
import jax.numpy as jnp
from jax import lax
from jax.experimental import pallas as pl
from jax.experimental.pallas import tpu as pltpu
from jax.sharding import Mesh, PartitionSpec as P

F32 = jnp.float32
BF16 = jnp.bfloat16
AXES = ("x", "ya", "yb", "yh", "z", "c")
DP = ("x", "ya", "yb")
Y = ("ya", "yb", "yh")
NX, NYA, NYB, NYH, NZ, NC = 4, 2, 2, 2, 8, 2
NYL = NYA * NYB
SEQ = ("yh", "z", "c")
SEQ_N = NYH * NZ * NC
C = 768
HALF = C // 2
L = 256
ROWS = 24
OWNERS = NYH * NZ
SUB = ROWS // (NX * NYB)
PIECE = 27
TOT = 24
MSG = 64
COUNT = L * SEQ_N * NX * NYL
NORM = float(COUNT) ** -0.5
SQRT_HALF = 0.7071067811865476
INV_SQRT_2PI = 0.3989422804014327
NT = (((1,), (1,)), ((), ()))
TN = (((0,), (0,)), ((), ()))
SPACES = {
    "s": pl.BlockSpec(memory_space=pltpu.SMEM),
    "v": pl.BlockSpec(memory_space=pltpu.VMEM),
    "a": pl.BlockSpec(memory_space=pl.ANY),
}


def call(kernel, out_shape, name, megabytes, spaces=None, out_specs=None, flops=0, size=1 << 20, scratch=()):
    params = pltpu.CompilerParams(vmem_limit_bytes=megabytes * 1024 * 1024)
    estimate = pl.CostEstimate(flops=flops, bytes_accessed=size, transcendentals=0)
    extra = {}
    if spaces is not None:
        extra["in_specs"] = [SPACES[letter] for letter in spaces]
    if out_specs is not None:
        extra["out_specs"] = out_specs
    return pl.pallas_call(
        kernel, out_shape=out_shape, compiler_params=params, cost_estimate=estimate, name=name,
        scratch_shapes=list(scratch), **extra,
    )


def fetch(sources, targets, sems):
    copies = [
        pltpu.make_async_copy(source, target, sems.at[i])
        for i, (source, target) in enumerate(zip(sources, targets))
    ]
    for copy in copies:
        copy.start()
    return copies


def spread(value, n):
    return jnp.broadcast_to(value[None], (n,) + value.shape)


def stats_kernel(inputs, message, block, sems):
    fetch([inputs], [block], sems)[0].wait()
    values = block[...].astype(F32)
    total = jnp.sum(values, axis=0, keepdims=True)
    off = values - total / L
    squares = jnp.sum(off * off, axis=0, keepdims=True)
    message[...] = spread(jnp.concatenate([total, squares], axis=0), NZ * NC)


def merged(parts, count):
    sums, squares = parts[:, 0, :], parts[:, 1, :]
    n = sums.shape[0]
    total = jnp.sum(sums, axis=0, keepdims=True)
    off = sums / count - total / (count * n)
    return total, jnp.sum(squares, axis=0, keepdims=True) + count * jnp.sum(off * off, axis=0, keepdims=True)


def merge_kernel(parts, message):
    total, squares = merged(parts[...], L)
    message[...] = spread(jnp.concatenate([total, squares], axis=0), NX * NYL * NYH)


def one_hot(channels):
    rows = lax.broadcasted_iota(jnp.int32, (C, channels.shape[1]), 0)
    return jnp.where(rows == channels[...], 1.0, 0.0).astype(BF16)


def normalised(block, vectors):
    return (block - vectors[0:1]) * vectors[1:2]


def half_gate(v):
    return 0.5 * (1.0 + lax.erf(v * SQRT_HALF))


def prepare_kernel(parts, gain, shift, source, inputs, vectors, chosen, act):
    total, squares = merged(parts[...], L * NZ * NC)
    mean = total / COUNT
    inv_std = lax.rsqrt(squares / COUNT + 1e-05)
    rows = jnp.concatenate([mean, inv_std, gain[...], shift[...]], axis=0)
    vectors[...] = rows
    pick = one_hot(source)
    some, rest = jnp.zeros((4, HALF), F32), rows
    for _ in range(3):
        part = rest.astype(BF16)
        some += jnp.dot(part, pick, preferred_element_type=F32)
        rest = rest - part.astype(F32)
    chosen[...] = some
    act[...] = activated(jnp.dot(inputs[...], pick, preferred_element_type=F32), some).astype(BF16)


def terms_kernel(place, chosen, act_own, source, mate, cot, outer, terms):
    low = place[0] == 0
    near = jnp.dot(mate[L : 2 * L], one_hot(source), preferred_element_type=F32)
    act = jnp.concatenate([act_own[...], activated(near, chosen[...]).astype(BF16)], axis=0)
    own, next_own, last_own = cot[...], mate[:L], outer[...]
    beyond = mate[2 * L :]
    cots = (
        (jnp.where(low, next_own, last_own), jnp.where(low, beyond, own)),
        (own, next_own),
        (jnp.where(low, last_own, next_own), jnp.where(low, own, beyond)),
    )
    for tap, pair in enumerate(cots):
        block = lax.dot_general(act, jnp.concatenate(pair, axis=0), TN, preferred_element_type=F32)
        terms[:, tap * C : (tap + 1) * C] = (block * NORM).astype(BF16)


def by_tap(kern, tap):
    return kern[:, tap].reshape(C, C)


def back_kernel(
    place, vectors, inputs_h, mate_h, cot_h, outer_h, kc, ko, channel, pre_grad, totals,
    inputs, mate, cot, outer, kern, sems,
):
    sources = [inputs_h, mate_h.at[:L], cot_h, outer_h, kc, ko]
    copies = fetch(sources, [inputs, mate, cot, outer, kern.at[:NZ], kern.at[NZ:]], sems)
    low = place[0] == 0
    pick = one_hot(channel)
    copies[0].wait()
    rows = vectors[...]
    normed = normalised(inputs[...].astype(F32), rows)
    v = rows[2:3] * normed + rows[3:4]
    slope = half_gate(v) + v * (INV_SQRT_2PI * jnp.exp(-0.5 * v * v))
    for copy in copies[1:]:
        copy.wait()
    taps = (
        jnp.where(low, mate[...], outer[...]),
        cot[...],
        jnp.where(low, outer[...], mate[...]),
    )
    total = jnp.zeros((L, C), F32)
    for tap, q in enumerate(taps):
        total += lax.dot_general(q, by_tap(kern, tap), NT, preferred_element_type=F32)
    high = total.astype(BF16)
    rest = (total - high.astype(F32)).astype(BF16)
    total = lax.dot_general(high, pick, NT, preferred_element_type=F32)
    total += lax.dot_general(rest, pick, NT, preferred_element_type=F32)
    grad = total * slope
    pre_grad[...] = grad
    totals[...] = jnp.concatenate(
        [jnp.sum(grad, axis=0, keepdims=True), jnp.sum(grad * normed, axis=0, keepdims=True)], axis=0
    )


def put_totals(totals, held):
    high = totals.astype(BF16).astype(F32)
    rows = jnp.concatenate([high, totals - high], axis=0)
    for tile in range(6):
        held[4 * tile : 4 * tile + 4] = rows[:, 128 * tile : 128 * tile + 128]
    return held[:TOT].astype(BF16)


def get_totals(held):
    rows = jnp.concatenate([held[4 * tile : 4 * tile + 4] for tile in range(6)], axis=1)
    return rows[0:2] + rows[2:4]


def first_kernel(got, totals, message, held):
    packed = put_totals(totals[...], held).astype(F32)
    parts = got[...].astype(F32)
    total = jnp.sum(parts, axis=0)
    zero = jnp.zeros((8, 128), F32)
    for l in range(NYA):
        for h in range(NYH):
            tiles = []
            for piece in range(PIECE):
                sub, tile = divmod(l * PIECE + piece, 18)
                row = sub * OWNERS + h * NZ
                tiles.append(total[row : row + 8, 128 * tile : 128 * tile + 128])
            tiles += [packed, zero, zero]
            message[l * NYH + h] = jnp.concatenate(tiles, axis=0).astype(BF16)


def second_kernel(got, message, held, line):
    total = jnp.sum(got[...].astype(F32), axis=0)
    held[...] = total[PIECE * 8 : PIECE * 8 + 32]
    packed = put_totals(get_totals(held), held).astype(F32)
    for piece in range(PIECE):
        line[:, TOT + piece, :] = total[piece * 8 : piece * 8 + 8]
    for z in range(NZ):
        line[z, :TOT] = packed
        line[z, TOT + PIECE :] = jnp.zeros((MSG - TOT - PIECE, 128), F32)
    message[...] = line[...].astype(BF16)


def third_kernel(got, message, held):
    total = jnp.sum(got[...].astype(F32), axis=0)
    held[...] = total[:32]
    packed = put_totals(get_totals(held), held)
    message[...] = spread(jnp.concatenate([packed, total[TOT:].astype(BF16)], axis=0), NX * NYL)


def last_kernel(
    got, vectors, inputs_h, cot_h, pre_h, grad_in, weights, gain_grad, shift_grad,
    inputs, cot, pre_grad, held, line, sems,
):
    copies = fetch([inputs_h, cot_h, pre_h], [inputs, cot, pre_grad], sems)
    total = jnp.zeros((32, 128), F32)
    for member in range(NX * NYL):
        part = got[member].astype(F32)
        line[...] = part
        x, l = divmod(member, NYL)
        a, b = divmod(l, NYB)
        if a == 0:
            total += part[:32]
        for piece in range(PIECE):
            sub, tile = divmod(a * PIECE + piece, 18)
            row = (x * NYB + b) * SUB + sub
            tap, lane = divmod(tile, 6)
            weights[tap, row : row + 1, 128 * lane : 128 * lane + 128] = line[TOT + piece : TOT + piece + 1]
    held[...] = total
    totals = get_totals(held)
    shift_grad[...] = (totals[0:1] * NORM).reshape(C)
    gain_grad[...] = (totals[1:2] * NORM).reshape(C)
    for copy in copies:
        copy.wait()
    rows = vectors[...]
    normed = normalised(inputs[...].astype(F32), rows)
    bn_grad = (rows[2:3] * rows[1:2]) * (
        pre_grad[...] - totals[0:1] / COUNT - normed * (totals[1:2] / COUNT)
    )
    grad_in[...] = (cot[...].astype(F32) + bn_grad).astype(BF16)


def activated(block, rows):
    v = rows[2:3] * normalised(block.astype(F32), rows) + rows[3:4]
    return v * half_gate(v)


def acts_kernel(place, vectors, inputs, mate_h, outer, channel, acts, mate, sems):
    copies = fetch([mate_h.at[L : 2 * L]], [mate], sems)
    rows = vectors[...]
    pick = one_hot(channel)
    low = place[0] == 0
    here = activated(inputs[...], rows).astype(BF16)
    away = jnp.where(place[1] == 1, activated(outer[...], rows), 0.0).astype(BF16)
    copies[0].wait()
    near = activated(mate[...], rows).astype(BF16)
    for tap, a in enumerate((jnp.where(low, away, near), here, jnp.where(low, near, away))):
        acts[tap] = jnp.dot(a, pick, preferred_element_type=F32).astype(BF16)


def forward_kernel(acts, inputs, kc, ko, output, kern, sems):
    copies = fetch([kc, ko], [kern.at[:NZ], kern.at[NZ:]], sems)
    total = inputs[...].astype(F32)
    for copy in copies:
        copy.wait()
    for tap in range(3):
        total += jnp.dot(acts[tap], by_tap(kern, tap), preferred_element_type=F32)
    output[...] = total.astype(BF16)


def shape(*dims, kind=F32):
    return jax.ShapeDtypeStruct(dims, kind)


def exchange(value, axes):
    return lax.all_to_all(value, axes, 0, 0, tiled=True)


def body(inputs, gain, shift, kernel, cotangent):
    yh, zi, ci = lax.axis_index("yh"), lax.axis_index("z"), lax.axis_index("c")
    inputs, cotangent = inputs[0], cotangent[0]
    gain, shift = gain[None], shift[None]
    seq = (yh * NZ + zi) * NC + ci
    has_outer = jnp.logical_and(seq > 0, seq < SEQ_N - 1).astype(jnp.int32)
    place = jnp.stack([ci, has_outer])
    order = jnp.arange(HALF)
    part, row, owner = order // (SUB * OWNERS), (order // OWNERS) % SUB, order % OWNERS
    source = ((owner * NC + ci) * ROWS + part * SUB + row)[None]
    order = jnp.arange(C)
    gp, gz = order // (NZ * NYH * ROWS), (order // (NYH * ROWS)) % NZ
    gy, gr = (order // ROWS) % NYH, order % ROWS
    channel = ((((gy + yh) % NYH * NZ + gz) * NC + (gp + ci) % NC) * ROWS + gr)[None]
    swap_c = [(0, 1), (1, 0)]
    swap_out = [(i, j) for i in range(1, SEQ_N - 1, 2) for i, j in ((i, i + 1), (i + 1, i))]
    swap_y = []
    for l in range(NYL):
        for h in range(NYH):
            y = 7 - (h * NYL + l)
            swap_y.append((l * NYH + h, (y % NYL) * NYH + y // NYL))

    own = kernel.transpose(1, 0, 2)
    other = lax.ppermute(own, Y, swap_y)
    stats = call(stats_kernel, shape(NZ * NC, 2, C), "stats", 8, "a", scratch=[
        pltpu.VMEM((L, C), BF16), pltpu.SemaphoreType.DMA((1,)),
    ])(inputs)
    stats, other, held_cot = lax.optimization_barrier((stats, other, cotangent))
    outer = lax.ppermute(held_cot, SEQ, swap_out)
    kernel_c = lax.all_gather(jnp.concatenate([own, other], axis=1), "z", axis=0, tiled=False)
    stats = exchange(stats, ("z", "c"))
    stats, outer, held_cot, held_in = lax.optimization_barrier((stats, outer, cotangent, inputs))
    stats = call(merge_kernel, shape(NX * NYL * NYH, 2, C), "merge", 8)(stats)
    mate = lax.ppermute(jnp.concatenate([held_cot, held_in, outer], axis=0), "c", swap_c)
    stats = exchange(stats, ("x",) + Y)

    vectors, chosen, act_own = call(
        prepare_kernel, (shape(4, C), shape(4, HALF), shape(L, HALF, kind=BF16)), "prepare", 24,
    )(stats, gain, shift, source, inputs)
    terms = call(
        terms_kernel, shape(HALF, 3 * C, kind=BF16), "terms", 24, "svvvvvv",
        flops=2 * 512 * HALF * C * 4, size=6 << 20,
    )(place, chosen, act_own, source, mate, cotangent, outer)
    terms = exchange(terms.reshape(NX * NYB, HALF // (NX * NYB), 3 * C), ("x", "yb"))

    kernel_o = lax.ppermute(kernel_c, "c", swap_c)
    kern = pltpu.VMEM((2 * NZ, 3, NYH * ROWS, C), BF16)
    pre_grad, totals = call(
        back_kernel, (shape(L, C), shape(2, C)), "back", 56, "svaaaaaav",
        flops=2 * L * C * C * 5, size=8 << 20,
        scratch=[
            pltpu.VMEM((L, C), BF16), pltpu.VMEM((L, C), BF16), pltpu.VMEM((L, C), BF16),
            pltpu.VMEM((L, C), BF16), kern, pltpu.SemaphoreType.DMA((6,)),
        ],
    )(place, vectors, inputs, mate, cotangent, outer, kernel_c, kernel_o, channel)
    totals = lax.psum(totals, "c")

    held = pltpu.VMEM((32, 128), F32)
    message = call(
        first_kernel, shape(NYA * NYH, 256, 128, kind=BF16), "first", 12, scratch=[held]
    )(terms, totals)
    message, late_in = lax.optimization_barrier((message, inputs))
    outer_in = lax.ppermute(late_in, SEQ, swap_out)
    got = exchange(message, ("ya", "yh"))
    message = call(
        second_kernel, shape(NZ, MSG, 128, kind=BF16), "second", 12,
        scratch=[held, pltpu.VMEM((NZ, MSG, 128), F32)],
    )(got)
    got = exchange(message, "z")
    acts = call(
        acts_kernel, shape(3, L, C, kind=BF16), "acts", 24, "svvavv", flops=2 * L * C * C * 3, size=2 << 20,
        scratch=[pltpu.VMEM((L, C), BF16), pltpu.SemaphoreType.DMA((1,))],
    )(place, vectors, inputs, mate, outer_in, channel)
    got, acts = lax.optimization_barrier((got, acts))
    message = call(third_kernel, shape(NX * NYL, MSG, 128, kind=BF16), "third", 12, scratch=[held])(got)
    got = exchange(message, DP)
    output = call(
        forward_kernel, shape(L, C, kind=BF16), "forward", 56, "vvaa", flops=2 * L * C * C * 3, size=6 << 20,
        scratch=[kern, pltpu.SemaphoreType.DMA((2,))],
    )(acts, inputs, kernel_c, kernel_o)
    got, output = lax.optimization_barrier((got, output))
    grad_in, weights, gain_grad, shift_grad = call(
        last_kernel,
        (shape(L, C, kind=BF16), shape(3, ROWS, C), shape(C), shape(C)), "last", 12, "vvaaa",
        scratch=[
            pltpu.VMEM((L, C), BF16), pltpu.VMEM((L, C), BF16), pltpu.VMEM((L, C), F32),
            held, pltpu.VMEM((MSG, 128), F32), pltpu.SemaphoreType.DMA((3,)),
        ],
    )(got, vectors, inputs, cotangent, pre_grad)
    return (output[None], grad_in[None], weights.transpose(1, 0, 2), gain_grad, shift_grad)


def solution(mesh):
    split_mesh = Mesh(mesh.devices.reshape(NX, NYA, NYB, NYH, NZ, NC), AXES)
    rows = P(DP, SEQ, None)
    return jax.shard_map(
        body,
        mesh=split_mesh,
        in_specs=(rows, P(), P(), P(SEQ, None, None), rows),
        out_specs=(rows, rows, P(SEQ, None, None), P(), P()),
        check_vma=False,
    )
```
